256 devices in a mesh: group: 4 (over x), dev: 64 (over y, z, core).
Axes of the slice: x: 4, y: 4, z: 8, core: 2. Of those that a mesh axis runs over, the one named last changes fastest.
Arguments:
- node_aggregate: bfloat16 [16384, 512], P(('group', 'dev')), may hold values from -6 to 6
- weight: bfloat16 [512, 512], replicated, may hold values from -0.25 to 0.25
- tiles: bfloat16 [8192, 128, 128], P(('group', 'dev'))
- tile_src: int32 [8192], P(('group', 'dev')), may hold values from 0 to 31
- tile_dst: int32 [8192], P(('group', 'dev')), may hold values from 0 to 1
- tile_count: int32 [256], P(('group', 'dev')), may hold values from 8 to 32
- pair_owner: int32 [2097152, 2], P(('group', 'dev')), may hold values from 0 to 63, all different within a row; in each aligned block of 8192 rows (0 to 8191, 8192 to 16383, ...) at most 512 rows name the same one
- pair_row: int32 [2097152, 2], P(('group', 'dev')), may hold values from 0 to 63
Outputs:
- feature_grad: bfloat16 [16384, 512], P(('group', 'dev'))
- weight_grad: float32 [512, 512], replicated
The draws below stay inside these ranges and needn't reach their ends.
Inputs may be any that keep to these rules, and one draw needn't show every extreme that they name: `pair_owner`: among the 16384 pair ends held by one device, at most 512 name one owner, and the two ends of a pair name different owners.
All inputs are finite; a program needn't handle non-finite values.
Results may differ from the reference program's by a relative error of at most 0.0032.
The reference program's roundings to bfloat16 on the way (of `hidden`, `pre_grad` and `agg_grad`) count: a program that leaves them out, or rounds other values in their place, can miss the bound.
Values may be sent and summed in bfloat16 or wider, within the bound.
No kernel may reach another device: no remote copies, remote signals or barrier semaphores. Data moves between devices by JAX's collectives and lax.ppermute only.
A program may use at most 128 MiB of HBM per device.

```python
import math
import jax
import jax.numpy as jnp
import numpy as np
from jax import lax

F = 512
TILE = 128
ROWS = 64
PAIRS_DEV = 8192
TILE_SLOTS = 32
CAP = 512
NODES = 16384
PAIRS = 2097152
SLOTS_ALL = 8192
N_GROUP = 4
N_DEV = 64


def draw_tiles(key, part):
    key = jax.random.fold_in(key, 11)
    key_live, key_value = jax.random.split(key, 2)
    shape = (TILE_SLOTS * N_GROUP * N_DEV, TILE, TILE)
    live_part = jax.random.uniform(key_live, shape, jnp.float32) < 0.25
    values = jnp.exp(jax.random.uniform(key_value, shape, jnp.float32, math.log(0.05), math.log(0.25)))
    return jnp.where(live_part, values, 0.0).astype(jnp.bfloat16)


def draw_tile_count(key, part):
    key = jax.random.fold_in(key, 23)
    key_count, key_full = jax.random.split(key)
    device_total = N_GROUP * N_DEV
    counts = jax.random.randint(key_count, (device_total,), TILE_SLOTS // 4, TILE_SLOTS + 1)
    busiest = jax.random.randint(key_full, (), 0, device_total)
    return counts.at[busiest].set(TILE_SLOTS).astype(jnp.int32)


def set_ends(values, key, smallest, largest):
    dims = values.shape
    place = [jax.random.randint(jax.random.fold_in(key, axis), (), 0, dims[axis]) for axis in range(len(dims))]
    values = values.at[tuple(place)].set(smallest)
    longest = dims.index(max(dims))
    place[longest] = (place[longest] + 1) % dims[longest]
    return values.at[tuple(place)].set(largest)


def steps_of(rng, shape, shards, low, high):
    gain, own = 1.0, jax.random.fold_in(rng, 6)
    for position, blocks in shards:
        heights = jnp.exp(jax.random.uniform(jax.random.fold_in(own, position), (blocks,), jnp.float32, low / len(shards), high / len(shards)))
        gain = gain * jnp.repeat(heights, shape[position] // blocks).reshape([-1 if axis == position else 1 for axis in range(len(shape))])
    return gain


def shared_out(own_key, own, number, rows, number_of, top, most, slope):
    ranking = jax.random.permutation(own_key, number_of)
    heavy_load, common = load_shares(number_of, rows * top, most, slope, True), load_shares(number_of, rows * top, most, slope, False)
    places = jnp.arange(number_of)

    def named(sizes, offset_by):
        used = int((sizes > 0).sum())
        fixed = max(1, used // 4)
        passed = fixed + (places - fixed + offset_by * (used - fixed)) % max(1, number_of - fixed)
        return jnp.zeros((number_of,), jnp.int32).at[ranking[jnp.where(places < fixed, places, passed)]].set(jnp.asarray(sizes, jnp.int32))

    sizes = jnp.where(number % 4 == 0, named(heavy_load, number // 4), named(common, number - number // 4 - 1))
    mixed = jax.random.permutation(jax.random.fold_in(own, 3), number_of)
    source_of, sink = mixed[0:number_of // 2 * 2:2], mixed[1:number_of // 2 * 2:2]
    slack = jnp.minimum(sizes[source_of] - 1, most - sizes[sink]) // 2
    slack = jnp.where((source_of == ranking[0]) | (sink == ranking[0]) | (sizes[sink] == 0), 0, jnp.maximum(slack, 0))
    passed = jax.random.randint(jax.random.fold_in(own, 4), (number_of // 2,), 0, 1 << 20) % (slack + 1)
    sizes = sizes.at[source_of].add(-passed).at[sink].add(passed)
    items = jnp.searchsorted(jnp.cumsum(sizes), jnp.arange(rows * top), side="right").astype(jnp.int32)
    listing = items.reshape(top, rows).T
    listing = listing[jax.random.permutation(jax.random.fold_in(own, 1), rows)]
    offset_by = jax.random.randint(jax.random.fold_in(own, 2), (rows, 1), 0, top)
    return jnp.take_along_axis(listing, (jnp.arange(top)[None, :] + offset_by) % top, axis=1)


def load_shares(count, total, reach, lean, full):
    weights = [(1 << 20) // math.isqrt(standing ** lean) + 1 for standing in range(1, count + 1)]
    largest = reach if full else min(reach, max(-(-total // count), total * weights[0] // sum(weights)))
    least = 1 if total - largest >= count - 1 else 0
    holding, surplus = [largest] + [least] * (count - 1), total - largest - least * (count - 1)
    while surplus > 0:
        movable = [i for i in range(1, count) if holding[i] < largest] or [i for i in range(1, count) if holding[i] < reach]
        pool, left = sum([weights[i] for i in movable]), surplus
        for i in movable:
            extra = min(reach - holding[i], max(1, left * weights[i] // pool), surplus)
            holding[i] = holding[i] + extra
            surplus = surplus - extra
    return np.array(holding)


def gaussian(key, extent, scale, most, cuts=(), kind=jnp.bfloat16):
    array = jax.random.normal(key, extent, jnp.float32) * scale
    if len(cuts) > 0:
        array = steps_of(key, extent, cuts, -0.22, 0.18) * array
    return jnp.clip(array, min=-most, max=most).astype(kind)


def setup_inputs(seed: int = 0) -> dict:
    arg_keys = jax.random.split(jax.random.key(seed), 9)
    node_aggregate = gaussian(arg_keys[0], (NODES, F), 1.0, 6.0, ((0, 256),))
    weight = gaussian(arg_keys[1], (F, F), F ** -0.5, 0.25)
    tiles = draw_tiles(jax.random.fold_in(arg_keys[8], 71), 0)
    tile_src = set_ends(jax.random.randint(arg_keys[3], (SLOTS_ALL,), 0, N_DEV * ROWS // TILE), jax.random.fold_in(arg_keys[3], 1), 0, (N_DEV * ROWS // TILE) - 1).astype(jnp.int32)
    tile_dst = set_ends(jax.random.randint(arg_keys[4], (SLOTS_ALL,), 0, N_GROUP * ROWS // TILE), jax.random.fold_in(arg_keys[4], 1), 0, (N_GROUP * ROWS // TILE) - 1).astype(jnp.int32)
    tile_count = draw_tile_count(jax.random.fold_in(arg_keys[8], 71), 0)
    pair_owner_keys = jax.random.split(jax.random.fold_in(arg_keys[6], 1), PAIRS // PAIRS_DEV)
    pair_owner_turns = jax.random.permutation(jax.random.fold_in(arg_keys[6], 3), PAIRS // PAIRS_DEV)
    pair_owner = jax.vmap(lambda own, number: shared_out(jax.random.fold_in(arg_keys[6], 2), own, number, PAIRS_DEV, N_DEV, 2, CAP, 2))(pair_owner_keys, pair_owner_turns).reshape((PAIRS, 2))
    pair_row = set_ends(jax.random.randint(arg_keys[7], (PAIRS, 2), 0, ROWS), jax.random.fold_in(arg_keys[7], 1), 0, ROWS - 1).astype(jnp.int32)
    return dict(node_aggregate=node_aggregate, weight=weight, tiles=tiles, tile_src=tile_src, tile_dst=tile_dst, tile_count=tile_count, pair_owner=pair_owner, pair_row=pair_row)


def activation(values):
    return jax.nn.gelu(values)

def reference(node_aggregate, weight, tiles, tile_src, tile_dst, tile_count, pair_owner, pair_row):
    device_total = N_GROUP * N_DEV
    quarter = N_DEV * ROWS
    pre_act = jnp.dot(node_aggregate, weight, preferred_element_type=jnp.float32)
    hidden, act_back = jax.vjp(activation, pre_act)
    hidden_b = hidden.astype(jnp.bfloat16)
    is_positive = (jnp.arange(PAIRS_DEV) < PAIRS_DEV // 5).astype(jnp.float32)
    end_scale = ROWS / (2.0 * PAIRS_DEV)

    def pair_step(running, pieces):
        owners, local_rows, device = pieces
        base = device // N_DEV * quarter
        node_a = (base + owners[:, 0] * ROWS + local_rows[:, 0]).astype(jnp.int32)
        node_b = (base + owners[:, 1] * ROWS + local_rows[:, 1]).astype(jnp.int32)
        head_rows = hidden_b[node_a].astype(jnp.float32)
        tail_rows = hidden_b[node_b].astype(jnp.float32)
        pair_score = lax.optimization_barrier(jnp.sum(head_rows * tail_rows, axis=1)) / math.sqrt(F)
        grad_score = (jax.nn.sigmoid(pair_score) - is_positive) * end_scale
        running = running.at[node_a].add(grad_score[:, None] * tail_rows)
        running = running.at[node_b].add(grad_score[:, None] * head_rows)
        return (running, None)
    hidden_grad, _ = lax.scan(pair_step, jnp.zeros((NODES, F), jnp.float32), (pair_owner.reshape(device_total, PAIRS_DEV, 2), pair_row.reshape(device_total, PAIRS_DEV, 2), jnp.arange(device_total, dtype=jnp.int32)))
    pre_grad = act_back(hidden_grad)[0].astype(jnp.bfloat16)
    weight_grad = jnp.dot(node_aggregate.T, pre_grad, preferred_element_type=jnp.float32)
    agg_grad = jnp.dot(pre_grad, weight.T, preferred_element_type=jnp.float32).astype(jnp.bfloat16)
    by_device = agg_grad.reshape(N_GROUP, N_DEV, ROWS, F)
    slot_ids = jnp.arange(TILE_SLOTS, dtype=jnp.int32)

    def tile_step(running, pieces):
        tile_block, src_ids, dst_ids, count, device = pieces
        group_id = device // N_DEV
        dev_id = device % N_DEV
        dst_rows = by_device[:, dev_id].reshape(N_GROUP * ROWS // TILE, TILE, F)
        dst_blocks = dst_rows[dst_ids].astype(jnp.float32)
        tile_terms = jnp.einsum('sij,sjf->sif', tile_block.astype(jnp.float32), dst_blocks)
        live_mask = (slot_ids < count).astype(jnp.float32)
        tile_terms = tile_terms * live_mask[:, None, None]
        running = running.at[group_id, src_ids].add(tile_terms)
        return (running, None)
    source_sum, _ = lax.scan(tile_step, jnp.zeros((N_GROUP, N_DEV * ROWS // TILE, TILE, F), jnp.float32), (tiles.reshape(device_total, TILE_SLOTS, TILE, TILE), tile_src.reshape(device_total, TILE_SLOTS), tile_dst.reshape(device_total, TILE_SLOTS), tile_count, jnp.arange(device_total, dtype=jnp.int32)))
    feature_grad = source_sum.reshape(NODES, F).astype(jnp.bfloat16)
    return (feature_grad, weight_grad)
```

```python
import functools
import math

import jax
import jax.numpy as jnp
from jax import lax
from jax.experimental import pallas as pl
from jax.experimental.pallas import tpu as pltpu
from jax.sharding import PartitionSpec as P

NX, NY, NZ, NC = 4, 4, 8, 2
NDEV = NY * NZ * NC
ROWS = 64
F = 512
CAP = 512
BF = jnp.bfloat16
F32 = jnp.float32
I32 = jnp.int32
POS = 4096.0
SUB = 256
SUBS = 8
NT = (((1,), (1,)), ((), ()))
TN = (((0,), (0,)), ((), ()))
VMEM = pl.BlockSpec(memory_space=pltpu.VMEM)
SMEM = pl.BlockSpec(memory_space=pltpu.SMEM)


def params(mib=48):
    return pltpu.CompilerParams(vmem_limit_bytes=mib << 20)


def activation(values):
    return jax.nn.gelu(values)


def bucket_kernel(owner_ref, row_ref, out_ref, acc):
    total = owner_ref.shape[1]
    positives = total // 5
    step = SUB * SUBS
    tri = (
        lax.broadcasted_iota(I32, (SUB, SUB), 0) < lax.broadcasted_iota(I32, (SUB, SUB), 1)
    ).astype(BF)
    acc[...] = jnp.zeros_like(acc)
    base = jnp.zeros((NDEV, 1), F32)
    for end in range(2):

        def body(j, base, end=end):
            ranks, parts = [], [[], [], [], []]
            for s in range(SUBS):
                start = pl.multiple_of(j * step + s * SUB, SUB)
                here = pl.ds(start, SUB)
                own = owner_ref[end : end + 1, here]
                same = lax.broadcasted_iota(I32, (NDEV, SUB), 0) == own
                hot = same.astype(F32)
                prefix = jnp.dot(hot.astype(BF), tri, preferred_element_type=F32)
                ranks.append(jnp.sum(hot * (prefix + base), axis=0, keepdims=True))
                base = base + jnp.sum(hot, axis=1, keepdims=True)
                place = start + lax.broadcasted_iota(I32, (1, SUB), 1)
                weight = jnp.where(place < positives, POS, 1.0)
                values = [
                    weight,
                    row_ref[end : end + 1, here].astype(F32),
                    owner_ref[1 - end : 2 - end, here].astype(F32),
                    row_ref[1 - end : 2 - end, here].astype(F32),
                ]
                for v in range(4):
                    parts[v].append((hot * values[v]).astype(BF))
            left = jnp.concatenate([jnp.concatenate(p, axis=1) for p in parts], axis=0)
            rank = jnp.concatenate(ranks, axis=1).astype(I32)
            right = (lax.broadcasted_iota(I32, (CAP, step), 0) == rank).astype(F32).astype(BF)
            acc[...] += lax.dot_general(left, right, NT, preferred_element_type=F32)
            return base

        base = lax.fori_loop(0, total // step, body, base)
    for v in range(4):
        out_ref[:, v * CAP : (v + 1) * CAP] = acc[v * NDEV : (v + 1) * NDEV, :].astype(BF)


def count_kernel(coord_ref, recv_ref, out_ref, left_at, right_at, weight_at):
    y, z, c = coord_ref[0], coord_ref[1], coord_ref[2]
    weight_at[...] = recv_ref[:, 0:CAP].astype(F32)
    own_row = recv_ref[:, CAP : 2 * CAP].astype(F32).astype(I32)
    owner = recv_ref[:, 2 * CAP : 3 * CAP].astype(F32).astype(I32)
    row = recv_ref[:, 3 * CAP : 4 * CAP].astype(F32).astype(I32)
    y_rel = ((owner >> 4) - y) & (NY - 1)
    z_rel = (((owner >> 1) & (NZ - 1)) - z) & (NZ - 1)
    c_rel = (owner & 1) ^ c
    left_at[...] = (c_rel * NY + y_rel) * ROWS + own_row
    right_at[...] = z_rel * ROWS + row
    out_ref[...] = jnp.zeros_like(out_ref)
    group = 4

    def body(g, carry):
        total = None
        for s in range(group):
            here = pl.ds(g * group + s, 1)
            spots = lax.broadcasted_iota(I32, (CAP, CAP), 0)
            left = jnp.where(spots == left_at[here, :], weight_at[here, :], 0.0).astype(BF)
            right = jnp.where(spots == right_at[here, :], 1.0, 0.0).astype(BF)
            term = lax.dot_general(left, right, NT, preferred_element_type=F32)
            total = term if total is None else total + term
        ones = jnp.floor(total * (1.0 / POS))
        out_ref[0] += total - (POS - 1.0) * ones
        out_ref[1] += ones
        return carry

    lax.fori_loop(0, NDEV // group, body, 0)


def grad_kernel(scale, own_ref, count_ref, *refs):
    pieces, out_ref = refs[:-1], refs[-1]
    own = own_ref[...]
    total = jnp.zeros((ROWS, F), F32)
    for k in range(NY * NC):
        nodes = pieces[k][...]
        score = lax.dot_general(own, nodes, NT, preferred_element_type=F32) / math.sqrt(F)
        here = slice(k * ROWS, (k + 1) * ROWS)
        grad = (count_ref[0, here, :] * jax.nn.sigmoid(score) - count_ref[1, here, :]) * scale
        high = grad.astype(BF)
        low = (grad - high.astype(F32)).astype(BF)
        total += jnp.dot(high, nodes, preferred_element_type=F32)
        total += jnp.dot(low, nodes, preferred_element_type=F32)
    out_ref[...] = total


def tiles_kernel(coord_ref, meta_ref, own_ref, other_ref, high_ref, low_ref, acc):
    y, z = coord_ref[0], coord_ref[1]
    slots = own_ref.shape[0]
    acc[...] = jnp.zeros_like(acc)
    for part, tiles_ref in enumerate((own_ref, other_ref)):

        def body(s, carry, part=part, tiles_ref=tiles_ref):
            block = meta_ref[part, s]
            dst = meta_ref[part, slots + s]
            y_rel = ((block >> 3) - y) & (NY - 1)
            z_rel = ((block & (NZ - 1)) - z) & (NZ - 1)
            rows = pl.ds(pl.multiple_of((y_rel * NZ + z_rel) * ROWS, ROWS), ROWS)
            columns = pl.ds(pl.multiple_of(part * 256 + dst * 128, 128), 128)
            acc[rows, columns] += tiles_ref[s].astype(F32)
            return carry

        lax.fori_loop(0, meta_ref[part, 2 * slots], body, 0)

    def split(k, carry):
        rows = pl.ds(pl.multiple_of(k * 128, 128), 128)
        value = acc[rows, :]
        high = value.astype(BF)
        high_ref[rows, :] = high
        low_ref[rows, :] = (value - high.astype(F32)).astype(BF)
        return carry

    lax.fori_loop(0, acc.shape[0] // 128, split, 0)


def spread_kernel(coord_ref, weight_ref, high_ref, low_ref, *refs):
    pre_refs, node_refs = refs[0:8], refs[8:12]
    terms_ref, keep_ref, send_refs = refs[12], refs[13], refs[14:17]
    pre, node = refs[17], refs[18]
    x = coord_ref[3]
    for k in range(NX):
        rows = pl.multiple_of(((x + k) & (NX - 1)) * ROWS, ROWS)
        node[pl.ds(rows, ROWS), :] = node_refs[k][...]
        for c in range(NC):
            pre[pl.ds(c * NX * ROWS + rows, ROWS), :] = pre_refs[c * NX + k][...]
    agg = lax.dot_general(pre[...], weight_ref[...], NT, preferred_element_type=F32).astype(BF)
    for k in (2, 1, 3, 0):
        rows = slice(k * NZ * ROWS, (k + 1) * NZ * ROWS)
        part = jnp.dot(high_ref[rows, :], agg, preferred_element_type=F32)
        part += jnp.dot(low_ref[rows, :], agg, preferred_element_type=F32)
        if k == 0:
            keep_ref[...] = part
        else:
            send_refs[k - 1][...] = part.astype(BF)
    mine = pre[0 : NX * ROWS, pl.ds(pl.multiple_of(x * 128, 128), 128)]
    terms_ref[...] = lax.dot_general(node[...], mine, TN, preferred_element_type=F32)


def dev_id(y, z, c):
    return ((y % NY) * NZ + z % NZ) * NC + c % NC


def shift(values, dy=0, dz=0, dc=0):
    pairs = [
        (dev_id(y, z, c), dev_id(y + dy, z + dz, c + dc))
        for y in range(NY)
        for z in range(NZ)
        for c in range(NC)
    ]
    return lax.ppermute(values, "dev", pairs)


def shift_all(values, dx, dc):
    pairs = [
        (x * NDEV + dev_id(y, z, c), ((x + dx) % NX) * NDEV + dev_id(y, z, c + dc))
        for x in range(NX)
        for y in range(NY)
        for z in range(NZ)
        for c in range(NC)
    ]
    return lax.ppermute(values, ("group", "dev"), pairs)


def pick(values, place):
    return lax.dynamic_index_in_dim(values, place, 0, keepdims=False)


def per_device(node_aggregate, weight, tiles, tile_src, tile_dst, tile_count, pair_owner, pair_row):
    pair_total = pair_owner.shape[0]
    slots = tiles.shape[0]
    device = lax.axis_index("dev")
    x = lax.axis_index("group")
    y, z, c = device // (NZ * NC), (device // NC) % NZ, device % NC
    coord = jnp.stack([y, z, c, x]).astype(I32)

    with jax.named_scope("hidden"):
        pre_act = jnp.dot(node_aggregate, weight, preferred_element_type=F32)
        hidden, act_back = jax.vjp(activation, pre_act)
        hidden_b = hidden.astype(BF)

    with jax.named_scope("hidden_gather"):
        along_z = [hidden_b] + [shift(hidden_b, dz=-k) for k in range(1, NZ)]
        ring = jnp.concatenate(along_z, axis=0)
        planes = [ring] + [shift(ring, dy=-k) for k in range(1, NY)]
        planes = planes + [shift(plane, dc=1) for plane in planes]

    with jax.named_scope("pair_exchange"):
        ends = pl.pallas_call(
            bucket_kernel,
            out_shape=jax.ShapeDtypeStruct((NDEV, 4 * CAP), BF),
            in_specs=[VMEM, VMEM],
            out_specs=VMEM,
            scratch_shapes=[pltpu.VMEM((4 * NDEV, CAP), F32)],
            compiler_params=params(),
            cost_estimate=pl.CostEstimate(flops=6_000_000_000, bytes_accessed=400_000, transcendentals=0),
            name="bucket",
        )(pair_owner.T, pair_row.T)
        received = lax.all_to_all(ends, "dev", 0, 0, tiled=True)
        counts = pl.pallas_call(
            count_kernel,
            out_shape=jax.ShapeDtypeStruct((2, NY * NC * ROWS, NZ * ROWS), F32),
            in_specs=[SMEM, VMEM],
            out_specs=VMEM,
            scratch_shapes=[
                pltpu.VMEM((NDEV, CAP), I32),
                pltpu.VMEM((NDEV, CAP), I32),
                pltpu.VMEM((NDEV, CAP), F32),
            ],
            compiler_params=params(),
            cost_estimate=pl.CostEstimate(flops=20_000_000_000, bytes_accessed=2_400_000, transcendentals=0),
            name="count",
        )(coord, received)

    with jax.named_scope("tile_matrix"):
        halves = tiles.reshape(slots, 2, ROWS, tiles.shape[2]).transpose(1, 0, 2, 3)
        own_half = pick(halves, c)
        other_half = shift(pick(halves, 1 - c), dc=1)
        meta = jnp.concatenate([tile_src, tile_dst, tile_count]).astype(I32)
        metas = jnp.stack([meta, shift(meta, dc=1)])
        high, low = pl.pallas_call(
            tiles_kernel,
            out_shape=[jax.ShapeDtypeStruct((NY * NZ * ROWS, 512), BF)] * 2,
            in_specs=[SMEM, SMEM, VMEM, VMEM],
            out_specs=[VMEM, VMEM],
            scratch_shapes=[pltpu.VMEM((NY * NZ * ROWS, 512), F32)],
            compiler_params=params(),
            cost_estimate=pl.CostEstimate(flops=2_000_000_000, bytes_accessed=5_000_000, transcendentals=0),
            name="tile_sum",
        )(coord, metas, own_half, other_half)
        nodes = [node_aggregate] + [shift_all(node_aggregate, -k, 0) for k in range(1, NX)]

    with jax.named_scope("hidden_grad"):
        hidden_grad = pl.pallas_call(
            functools.partial(grad_kernel, ROWS / (2.0 * pair_total)),
            out_shape=jax.ShapeDtypeStruct((ROWS, F), F32),
            in_specs=[VMEM] * (2 + len(planes)),
            out_specs=VMEM,
            compiler_params=params(),
            cost_estimate=pl.CostEstimate(flops=1_000_000_000, bytes_accessed=6_000_000, transcendentals=262144),
            name="pair_grad",
        )(hidden_b, counts, *planes)
        pre_grad = act_back(hidden_grad)[0].astype(BF)

    with jax.named_scope("spread"):
        pre_parts = [
            pre_grad if dx == 0 and dc == 0 else shift_all(pre_grad, -dx, dc)
            for dc in range(NC)
            for dx in range(NX)
        ]
        terms, keep, *send = pl.pallas_call(
            spread_kernel,
            out_shape=[
                jax.ShapeDtypeStruct((F, 128), F32),
                jax.ShapeDtypeStruct((NZ * ROWS, F), F32),
            ]
            + [jax.ShapeDtypeStruct((NZ * ROWS, F), BF)] * 3,
            in_specs=[SMEM] + [VMEM] * 15,
            out_specs=[VMEM] * 5,
            scratch_shapes=[pltpu.VMEM((NC * NX * ROWS, F), BF), pltpu.VMEM((NX * ROWS, F), BF)],
            compiler_params=params(),
            cost_estimate=pl.CostEstimate(flops=3_000_000_000, bytes_accessed=8_000_000, transcendentals=0),
            name="spread",
        )(coord, weight, high, low, *pre_parts, *nodes)

    with jax.named_scope("feature_sum"):
        total = keep
        for k in (2, 1, 3):
            total = total + shift(send[k - 1], dy=k).astype(F32)
        rows = total.reshape(NZ, ROWS, F)
        feature = rows[0]
        for k in (4, 3, 5, 2, 6, 1, 7):
            feature = feature + shift(rows[k].astype(BF), dz=k).astype(F32)
        feature_grad = feature.astype(BF)

    with jax.named_scope("weight_sum"):
        halves = terms.reshape(NC, F // NC, 128)
        part = pick(halves, c) + shift(pick(halves, 1 - c), dc=1)
        quarters = part.reshape(NY, F // (NC * NY), 128)
        part = pick(quarters, y)
        for k in range(1, NY):
            part = part + shift(pick(quarters, (y + k) % NY), dy=k)
        ring = jnp.zeros((NZ,) + part.shape, F32)
        ring = lax.dynamic_update_index_in_dim(ring, part, z, 0)
        for k in range(1, NZ):
            ring = lax.dynamic_update_index_in_dim(ring, shift(part, dz=k), (z - k) % NZ, 0)
        total = ring[0]
        for k in range(1, NZ):
            total = total + ring[k]
        blocks = jnp.zeros((NY, F // (NC * NY), 128), F32)
        blocks = lax.dynamic_update_index_in_dim(blocks, total, y, 0)
        for k in range(1, NY):
            blocks = lax.dynamic_update_index_in_dim(blocks, shift(total, dy=-k), (y + k) % NY, 0)
        column = blocks.reshape(F // NC, 128)
        columns = jnp.zeros((NX, F // NC, 128), F32)
        columns = lax.dynamic_update_index_in_dim(columns, column, x, 0)
        for k in range(1, NX):
            columns = lax.dynamic_update_index_in_dim(columns, shift_all(column, -k, 0), (x + k) % NX, 0)
        half = columns.transpose(1, 0, 2).reshape(F // NC, F)
        other = shift(half, dc=1)
        first = c == 0
        weight_grad = jnp.concatenate(
            [jnp.where(first, half, other), jnp.where(first, other, half)], axis=0
        )
    return (feature_grad, weight_grad)


def solution(mesh):
    spec = P(("group", "dev"))
    return jax.shard_map(
        per_device,
        mesh=mesh,
        in_specs=(
            P(("group", "dev"), None),
            P(),
            P(("group", "dev"), None, None),
            spec,
            spec,
            spec,
            P(("group", "dev"), None),
            P(("group", "dev"), None),
        ),
        out_specs=(P(("group", "dev"), None), P()),
        check_vma=False,
    )
```

```python
import functools
import math

import jax
import jax.numpy as jnp
from jax import lax
from jax.experimental import pallas as pl
from jax.experimental.pallas import tpu as pltpu
from jax.sharding import Mesh, PartitionSpec as P

NX, NY, NZ, NC = 4, 4, 8, 2
NDEV = NY * NZ * NC
ROWS = 64
F = 512
CAP = 512
BF = jnp.bfloat16
F32 = jnp.float32
I32 = jnp.int32
POS = 4096.0
SUB = 256
SUBS = 8
NT = (((1,), (1,)), ((), ()))
TN = (((0,), (0,)), ((), ()))
VMEM = pl.BlockSpec(memory_space=pltpu.VMEM)
SMEM = pl.BlockSpec(memory_space=pltpu.SMEM)
ANY = pl.BlockSpec(memory_space=pl.ANY)


TOKEN = jax.ShapeDtypeStruct((8, 128), F32)


def params(mib=16):
    return pltpu.CompilerParams(vmem_limit_bytes=mib << 20)


def activation(values):
    return jax.nn.gelu(values)


def bucket_kernel(owner_ref, row_ref, out_ref, token_ref, acc):
    token_ref[...] = jnp.zeros_like(token_ref)
    total = owner_ref.shape[1]
    positives = total // 5
    step = SUB * SUBS
    tri = (
        lax.broadcasted_iota(I32, (SUB, SUB), 0) < lax.broadcasted_iota(I32, (SUB, SUB), 1)
    ).astype(BF)
    acc[...] = jnp.zeros_like(acc)
    base = jnp.zeros((NDEV, 1), F32)
    for end in range(2):

        def body(j, base, end=end):
            ranks, parts = [], [[], [], [], []]
            for s in range(SUBS):
                start = pl.multiple_of(j * step + s * SUB, SUB)
                here = pl.ds(start, SUB)
                own = owner_ref[end : end + 1, here]
                same = lax.broadcasted_iota(I32, (NDEV, SUB), 0) == own
                hot = same.astype(F32)
                prefix = jnp.dot(hot.astype(BF), tri, preferred_element_type=F32)
                ranks.append(jnp.sum(hot * (prefix + base), axis=0, keepdims=True))
                base = base + jnp.sum(hot, axis=1, keepdims=True)
                place = start + lax.broadcasted_iota(I32, (1, SUB), 1)
                weight = jnp.where(place < positives, POS, 1.0)
                values = [
                    weight,
                    row_ref[end : end + 1, here].astype(F32),
                    owner_ref[1 - end : 2 - end, here].astype(F32),
                    row_ref[1 - end : 2 - end, here].astype(F32),
                ]
                for v in range(4):
                    parts[v].append((hot * values[v]).astype(BF))
            left = jnp.concatenate([jnp.concatenate(p, axis=1) for p in parts], axis=0)
            rank = jnp.concatenate(ranks, axis=1).astype(I32)
            right = (lax.broadcasted_iota(I32, (CAP, step), 0) == rank).astype(F32).astype(BF)
            acc[...] += lax.dot_general(left, right, NT, preferred_element_type=F32)
            return base

        base = lax.fori_loop(0, total // step, body, base)
    for v in range(4):
        out_ref[:, v * CAP : (v + 1) * CAP] = acc[v * NDEV : (v + 1) * NDEV, :].astype(BF)


def count_kernel(first, coord_ref, _, recv_ref, *refs):
    out_ref, token_ref, left_at, right_at, weight_at = refs[-5:]
    token_ref[...] = jnp.zeros_like(token_ref)
    y, c = coord_ref[0], coord_ref[1]
    weight_at[...] = recv_ref[:, 0:CAP].astype(F32)
    own_row = recv_ref[:, CAP : 2 * CAP].astype(F32).astype(I32)
    owner = recv_ref[:, 2 * CAP : 3 * CAP].astype(F32).astype(I32)
    row = recv_ref[:, 3 * CAP : 4 * CAP].astype(F32).astype(I32)
    piece = ((owner & 1) ^ c) * NY + (((owner >> 4) - y) & (NY - 1))
    left_at[...] = piece * ROWS + own_row
    right_at[...] = ((owner >> 1) & (NZ - 1)) * ROWS + row
    if first:
        out_ref[...] = jnp.zeros_like(out_ref)
    else:
        out_ref[...] = refs[0][...]
    group = 4

    def body(g, carry):
        total = None
        for s in range(group):
            here = pl.ds(g * group + s, 1)
            spots = lax.broadcasted_iota(I32, (CAP, CAP), 0)
            left = jnp.where(spots == left_at[here, :], weight_at[here, :], 0.0).astype(BF)
            right = jnp.where(spots == right_at[here, :], 1.0, 0.0).astype(BF)
            term = lax.dot_general(left, right, NT, preferred_element_type=F32)
            total = term if total is None else total + term
        ones = jnp.floor(total * (1.0 / POS))
        out_ref[0] += total - (POS - 1.0) * ones
        out_ref[1] += ones
        return carry

    half = NDEV // group // 2
    lax.fori_loop(0 if first else half, half if first else 2 * half, body, 0)


def grad_kernel(scale, _, own_ref, count_ref, *refs):
    pieces, out_ref = refs[:-1], refs[-1]
    own = own_ref[...]
    total = jnp.zeros((ROWS, F), F32)
    for k in range(NY * NC):
        nodes = pieces[k][...]
        score = lax.dot_general(own, nodes, NT, preferred_element_type=F32) / math.sqrt(F)
        here = slice(k * ROWS, (k + 1) * ROWS)
        grad = (count_ref[0, here, :] * jax.nn.sigmoid(score) - count_ref[1, here, :]) * scale
        high = grad.astype(BF)
        low = (grad - high.astype(F32)).astype(BF)
        total += jnp.dot(high, nodes, preferred_element_type=F32)
        total += jnp.dot(low, nodes, preferred_element_type=F32)
    out_ref[...] = total


def tiles_kernel(meta_ref, own_ref, other_ref, high_ref, low_ref, token_ref, acc):
    token_ref[...] = jnp.zeros_like(token_ref)
    slots = own_ref.shape[0]
    acc[...] = jnp.zeros_like(acc)
    for part, tiles_ref in enumerate((own_ref, other_ref)):

        def body(s, carry, part=part, tiles_ref=tiles_ref):
            rows = pl.ds(pl.multiple_of(meta_ref[part, s] * ROWS, ROWS), ROWS)
            dst = meta_ref[part, slots + s]
            columns = pl.ds(pl.multiple_of(part * 256 + dst * 128, 128), 128)
            acc[rows, columns] += tiles_ref[s].astype(F32)
            return carry

        lax.fori_loop(0, meta_ref[part, 2 * slots], body, 0)

    def split(k, carry):
        rows = pl.ds(pl.multiple_of(k * 128, 128), 128)
        value = acc[rows, :]
        high = value.astype(BF)
        high_ref[rows, :] = high
        low_ref[rows, :] = (value - high.astype(F32)).astype(BF)
        return carry

    lax.fori_loop(0, acc.shape[0] // 128, split, 0)


def spread_kernel(coord_ref, weight_ref, high_ref, low_ref, pre_ref, *refs):
    out_refs, token_ref, pre = refs[:-2], refs[-2], refs[-1]
    token_ref[...] = jnp.zeros_like(token_ref)
    y, c = coord_ref[0], coord_ref[1]
    for k in range(NX * NC):
        place = pl.multiple_of(((k % NC) ^ c) * NX * ROWS + (k // NC) * ROWS, ROWS)
        pre[pl.ds(place, ROWS), :] = pre_ref[k]
    agg = lax.dot_general(pre[...], weight_ref[...], NT, preferred_element_type=F32).astype(BF)
    size = NZ * ROWS
    for k in range(NY):
        rows = pl.ds(pl.multiple_of(((y + k) & (NY - 1)) * size, size), size)
        part = jnp.dot(high_ref[rows, :], agg, preferred_element_type=F32)
        part += jnp.dot(low_ref[rows, :], agg, preferred_element_type=F32)
        out_refs[k][...] = part.astype(out_refs[k].dtype)


def terms_kernel(_, pre_ref, node_ref, terms_ref):
    total = jnp.zeros(terms_ref.shape, F32)
    for k in range(NX * NC):
        total += lax.dot_general(node_ref[k], pre_ref[k], TN, preferred_element_type=F32)
    terms_ref[...] = total


def swap(values):
    return lax.ppermute(values, "c", [(0, 1), (1, 0)])


def shift(values, axis, size, step):
    return lax.ppermute(values, axis, [(i, (i + step) % size) for i in range(size)])


def exchange(values, axes):
    return lax.all_to_all(values, axes, 0, 0, tiled=True)


def gather(values, axes, size):
    return exchange(jnp.broadcast_to(values[None], (size,) + values.shape), axes)


def pick(values, place):
    return lax.dynamic_index_in_dim(values, place, 0, keepdims=False)


def count(coord, token, received, *counted):
    return pl.pallas_call(
        functools.partial(count_kernel, not counted),
        out_shape=[jax.ShapeDtypeStruct((2, NY * NC * ROWS, NZ * ROWS), F32), TOKEN],
        in_specs=[SMEM, ANY, VMEM] + [VMEM] * len(counted),
        out_specs=[VMEM, VMEM],
        scratch_shapes=[
            pltpu.VMEM((NDEV, CAP), I32),
            pltpu.VMEM((NDEV, CAP), I32),
            pltpu.VMEM((NDEV, CAP), F32),
        ],
        compiler_params=params(),
        cost_estimate=pl.CostEstimate(flops=12_000_000_000, bytes_accessed=2_400_000, transcendentals=0),
        name="count",
    )(coord, token, received, *counted)


def per_device(node_aggregate, weight, tiles, tile_src, tile_dst, tile_count, pair_owner, pair_row):
    pair_total = pair_owner.shape[0]
    slots = tiles.shape[0]
    c = lax.axis_index("c")
    coord = jnp.stack([lax.axis_index("y"), c]).astype(I32)

    with jax.named_scope("hidden"):
        pre_act = jnp.dot(node_aggregate, weight, preferred_element_type=F32)
        hidden, act_back = jax.vjp(activation, pre_act)
        hidden_b = hidden.astype(BF)

    with jax.named_scope("pair_exchange"):
        ring = gather(hidden_b, "z", NZ).reshape(NZ * ROWS, F)
        ends, token = pl.pallas_call(
            bucket_kernel,
            out_shape=[jax.ShapeDtypeStruct((NDEV, 4 * CAP), BF), TOKEN],
            in_specs=[VMEM, VMEM],
            out_specs=[VMEM, VMEM],
            scratch_shapes=[pltpu.VMEM((4 * NDEV, CAP), F32)],
            compiler_params=params(),
            cost_estimate=pl.CostEstimate(flops=9_000_000_000, bytes_accessed=400_000, transcendentals=0),
            name="bucket",
        )(pair_owner.T, pair_row.T)
        ring, ends = lax.optimization_barrier((ring, ends))
        planes = [ring] + [shift(ring, "y", NY, -k) for k in range(1, NY)]
        received = exchange(ends, ("y", "z", "c"))
        counted, token = count(coord, token, received)
        columns = node_aggregate.reshape(ROWS, NX * NC, ROWS).transpose(1, 0, 2)
        planes, columns, token = lax.optimization_barrier((planes, columns, token))
        planes = planes + [swap(plane) for plane in planes]
        counted, _ = count(coord, token, received, counted)

    with jax.named_scope("tile_matrix"):
        halves = tiles.reshape(slots, 2, ROWS, tiles.shape[2]).transpose(1, 0, 2, 3)
        own_half = pick(halves, c)
        other_half = swap(pick(halves, 1 - c))
        meta = jnp.concatenate([tile_src, tile_dst, tile_count]).astype(I32)
        metas = jnp.stack([meta, swap(meta)])
        high, low, token = pl.pallas_call(
            tiles_kernel,
            out_shape=[jax.ShapeDtypeStruct((NY * NZ * ROWS, 512), BF)] * 2 + [TOKEN],
            in_specs=[SMEM, VMEM, VMEM],
            out_specs=[VMEM] * 3,
            scratch_shapes=[pltpu.VMEM((NY * NZ * ROWS, 512), F32)],
            compiler_params=params(),
            cost_estimate=pl.CostEstimate(flops=3_000_000_000, bytes_accessed=5_000_000, transcendentals=0),
            name="tile_sum",
        )(metas, own_half, other_half)
        nodes = exchange(columns, ("x", "c"))

    with jax.named_scope("hidden_grad"):
        own, token, nodes = lax.optimization_barrier((hidden_b, token, nodes))
        hidden_grad = pl.pallas_call(
            functools.partial(grad_kernel, ROWS / (2.0 * pair_total)),
            out_shape=jax.ShapeDtypeStruct((ROWS, F), F32),
            in_specs=[ANY] + [VMEM] * (2 + len(planes)),
            out_specs=VMEM,
            compiler_params=params(),
            cost_estimate=pl.CostEstimate(flops=5_000_000_000, bytes_accessed=6_000_000, transcendentals=262144),
            name="pair_grad",
        )(token, own, counted, *planes)
        pre_grad = act_back(hidden_grad)[0].astype(BF)

    with jax.named_scope("spread"):
        pre_parts = gather(pre_grad, ("x", "c"), NX * NC)
        keep, *send, token = pl.pallas_call(
            spread_kernel,
            out_shape=[
                jax.ShapeDtypeStruct((NZ * ROWS, F), dtype) for dtype in (F32,) + (BF,) * (NY - 1)
            ]
            + [TOKEN],
            in_specs=[SMEM] + [VMEM] * 4,
            out_specs=[VMEM] * (NY + 1),
            scratch_shapes=[pltpu.VMEM((NC * NX * ROWS, F), BF)],
            compiler_params=params(),
            cost_estimate=pl.CostEstimate(flops=5_000_000_000, bytes_accessed=8_000_000, transcendentals=0),
            name="spread",
        )(coord, weight, high, low, pre_parts)
        pre_parts, token = lax.optimization_barrier((pre_parts, token))
        terms = pl.pallas_call(
            terms_kernel,
            out_shape=jax.ShapeDtypeStruct((ROWS, F), F32),
            in_specs=[ANY] + [VMEM] * 2,
            out_specs=VMEM,
            compiler_params=params(),
            cost_estimate=pl.CostEstimate(flops=1_000_000_000, bytes_accessed=700_000, transcendentals=0),
            name="weight_terms",
        )(token, pre_parts, nodes)

    with jax.named_scope("sums"):
        chips = NY * NZ
        part = keep
        for k in (2, 1, 3):
            part = part + shift(send[k - 1], "y", NY, k).astype(F32)
        part = part.astype(BF)
        shares = exchange(terms.reshape(chips, ROWS // chips, F), ("y", "z"))
        share = jnp.sum(shares, axis=0)
        block = gather(share, ("y", "z"), chips).reshape(ROWS, F)
        part, block = lax.optimization_barrier((part, block))
        rings = exchange(part.reshape(NZ, ROWS, F), "z").astype(F32)
        other = swap(block)
        low_first = c == 0
        pair = jnp.stack([jnp.where(low_first, block, other), jnp.where(low_first, other, block)])
        x = lax.axis_index("x")
        blocks = jnp.zeros((NX,) + pair.shape, F32)
        blocks = lax.dynamic_update_index_in_dim(blocks, pair, x, 0)
        for k in range(1, NX):
            blocks = lax.dynamic_update_index_in_dim(
                blocks, shift(pair, "x", NX, -k), (x + k) & (NX - 1), 0
            )
        weight_grad = blocks.reshape(F, F)
        feature_grad = jnp.sum(rings, axis=0).astype(BF)
    return (feature_grad, weight_grad)


def solution(mesh):
    grid = Mesh(mesh.devices.reshape(NX, NY, NZ, NC), ("x", "y", "z", "c"))
    split = P(("x", "y", "z", "c"))
    return jax.shard_map(
        per_device,
        mesh=grid,
        in_specs=(split, P(), split, split, split, split, split, split),
        out_specs=(split, P()),
        check_vma=False,
    )
```

```python
import functools
import math

import jax
import jax.numpy as jnp
from jax import lax
from jax.experimental import pallas as pl
from jax.experimental.pallas import tpu as pltpu
from jax.sharding import Mesh, PartitionSpec as P

NX, NY, NZ, NC = 4, 4, 8, 2
NDEV = NY * NZ * NC
ROWS = 64
F = 512
CAP = 512
BF = jnp.bfloat16
F32 = jnp.float32
I32 = jnp.int32
POS = 4096.0
SUB = 256
SUBS = 8
NT = (((1,), (1,)), ((), ()))
TN = (((0,), (0,)), ((), ()))
VMEM = pl.BlockSpec(memory_space=pltpu.VMEM)
SMEM = pl.BlockSpec(memory_space=pltpu.SMEM)
ANY = pl.BlockSpec(memory_space=pl.ANY)


TOKEN = jax.ShapeDtypeStruct((8, 128), F32)


def params(mib=16):
    return pltpu.CompilerParams(vmem_limit_bytes=mib << 20)


def activation(values):
    return jax.nn.gelu(values)


def bucket_kernel(owner_ref, row_ref, out_ref, token_ref, acc):
    token_ref[...] = jnp.zeros_like(token_ref)
    total = owner_ref.shape[1]
    positives = total // 5
    step = SUB * SUBS
    tri = (
        lax.broadcasted_iota(I32, (SUB, SUB), 0) < lax.broadcasted_iota(I32, (SUB, SUB), 1)
    ).astype(BF)
    acc[...] = jnp.zeros_like(acc)
    base = jnp.zeros((NDEV, 1), F32)
    for end in range(2):

        def body(j, base, end=end):
            ranks, parts = [], [[], [], [], []]
            for s in range(SUBS):
                start = pl.multiple_of(j * step + s * SUB, SUB)
                here = pl.ds(start, SUB)
                own = owner_ref[end : end + 1, here]
                same = lax.broadcasted_iota(I32, (NDEV, SUB), 0) == own
                hot = same.astype(F32)
                prefix = jnp.dot(hot.astype(BF), tri, preferred_element_type=F32)
                ranks.append(jnp.sum(hot * (prefix + base), axis=0, keepdims=True))
                base = base + jnp.sum(hot, axis=1, keepdims=True)
                place = start + lax.broadcasted_iota(I32, (1, SUB), 1)
                weight = jnp.where(place < positives, POS, 1.0)
                values = [
                    weight,
                    row_ref[end : end + 1, here].astype(F32),
                    owner_ref[1 - end : 2 - end, here].astype(F32),
                    row_ref[1 - end : 2 - end, here].astype(F32),
                ]
                for v in range(4):
                    parts[v].append((hot * values[v]).astype(BF))
            left = jnp.concatenate([jnp.concatenate(p, axis=1) for p in parts], axis=0)
            rank = jnp.concatenate(ranks, axis=1).astype(I32)
            right = (lax.broadcasted_iota(I32, (CAP, step), 0) == rank).astype(F32).astype(BF)
            acc[...] += lax.dot_general(left, right, NT, preferred_element_type=F32)
            return base

        base = lax.fori_loop(0, total // step, body, base)
    for v in range(4):
        out_ref[:, v * CAP : (v + 1) * CAP] = acc[v * NDEV : (v + 1) * NDEV, :].astype(BF)


def count_kernel(first, coord_ref, _, recv_ref, *refs):
    out_ref, token_ref, left_at, right_at, weight_at = refs[-5:]
    token_ref[...] = jnp.zeros_like(token_ref)
    y, c = coord_ref[0], coord_ref[1]
    weight_at[...] = recv_ref[:, 0:CAP].astype(F32)
    own_row = recv_ref[:, CAP : 2 * CAP].astype(F32).astype(I32)
    owner = recv_ref[:, 2 * CAP : 3 * CAP].astype(F32).astype(I32)
    row = recv_ref[:, 3 * CAP : 4 * CAP].astype(F32).astype(I32)
    piece = ((owner & 1) ^ c) * NY + (((owner >> 4) - y) & (NY - 1))
    left_at[...] = piece * ROWS + own_row
    right_at[...] = ((owner >> 1) & (NZ - 1)) * ROWS + row
    if first:
        out_ref[...] = jnp.zeros_like(out_ref)
    else:
        out_ref[...] = refs[0][...]
    group = 7
    groups = NDEV // group
    half = (groups + 1) // 2

    def add(start, size):
        spots = lax.broadcasted_iota(I32, (CAP, CAP), 0)
        left, right = [], []
        for s in range(size):
            here = pl.ds(start + s, 1)
            left.append(jnp.where(spots == left_at[here, :], weight_at[here, :], 0.0).astype(BF))
            right.append(jnp.where(spots == right_at[here, :], 1.0, 0.0).astype(BF))
        total = lax.dot_general(
            jnp.concatenate(left, axis=1), jnp.concatenate(right, axis=1), NT, preferred_element_type=F32
        )
        ones = jnp.floor(total * (1.0 / POS))
        out_ref[0] += total - (POS - 1.0) * ones
        out_ref[1] += ones

    def body(g, carry):
        add(g * group, group)
        return carry

    lax.fori_loop(0 if first else half, half if first else groups, body, 0)
    if not first:
        add(groups * group, NDEV - groups * group)


def grad_kernel(scale, _, own_ref, count_ref, *refs):
    pieces, out_ref = refs[:-1], refs[-1]
    own = own_ref[...]
    total = jnp.zeros((ROWS, F), F32)
    for k in range(NY * NC):
        nodes = pieces[k][...]
        score = lax.dot_general(own, nodes, NT, preferred_element_type=F32) / math.sqrt(F)
        here = slice(k * ROWS, (k + 1) * ROWS)
        grad = (count_ref[0, here, :] * jax.nn.sigmoid(score) - count_ref[1, here, :]) * scale
        high = grad.astype(BF)
        low = (grad - high.astype(F32)).astype(BF)
        total += jnp.dot(high, nodes, preferred_element_type=F32)
        total += jnp.dot(low, nodes, preferred_element_type=F32)
    out_ref[...] = total


def tiles_kernel(meta_ref, own_ref, other_ref, high_ref, low_ref, token_ref, acc):
    token_ref[...] = jnp.zeros_like(token_ref)
    slots = own_ref.shape[0]
    acc[...] = jnp.zeros_like(acc)
    for part, tiles_ref in enumerate((own_ref, other_ref)):

        def body(s, carry, part=part, tiles_ref=tiles_ref):
            rows = pl.ds(pl.multiple_of(meta_ref[part, s] * ROWS, ROWS), ROWS)
            dst = meta_ref[part, slots + s]
            columns = pl.ds(pl.multiple_of(part * 256 + dst * 128, 128), 128)
            acc[rows, columns] += tiles_ref[s].astype(F32)
            return carry

        lax.fori_loop(0, meta_ref[part, 2 * slots], body, 0)

    def split(k, carry):
        rows = pl.ds(pl.multiple_of(k * 128, 128), 128)
        value = acc[rows, :]
        high = value.astype(BF)
        high_ref[rows, :] = high
        low_ref[rows, :] = (value - high.astype(F32)).astype(BF)
        return carry

    lax.fori_loop(0, acc.shape[0] // 128, split, 0)


def spread_kernel(coord_ref, _, weight_ref, high_ref, low_ref, *refs):
    pre_refs, out_refs, token_ref, pre = refs[:8], refs[8:-2], refs[-2], refs[-1]
    token_ref[...] = jnp.zeros_like(token_ref)
    y, x = coord_ref[0], coord_ref[2]
    for k in range(NC * NX):
        dc, dx = k // NX, k % NX
        place = pl.multiple_of((dc * NX + ((x + dx) & (NX - 1))) * ROWS, ROWS)
        pre[pl.ds(place, ROWS), :] = pre_refs[k][...]
    agg = lax.dot_general(pre[...], weight_ref[...], NT, preferred_element_type=F32).astype(BF)
    size = NZ * ROWS
    for k in range(NY):
        rows = pl.ds(pl.multiple_of(((y + k) & (NY - 1)) * size, size), size)
        part = jnp.dot(high_ref[rows, :], agg, preferred_element_type=F32)
        part += jnp.dot(low_ref[rows, :], agg, preferred_element_type=F32)
        out_refs[k][...] = part.astype(out_refs[k].dtype)


def terms_kernel(coord_ref, node_ref, *refs):
    pre_refs, out_refs, token_ref, terms = refs[:8], refs[8:12], refs[12], refs[13]
    token_ref[...] = jnp.zeros_like(token_ref)
    y, c, x = coord_ref[0], coord_ref[1], coord_ref[2]
    total = jnp.zeros(terms.shape, F32)
    for k in range(NC * NX):
        dc, dx = k // NX, k % NX
        node = node_ref[((x + dx) & (NX - 1)) * NC + (c ^ dc)]
        total += lax.dot_general(node, pre_refs[k][...], TN, preferred_element_type=F32)
    terms[...] = total
    size = ROWS // NY
    for k in range(NY):
        rows = pl.ds(pl.multiple_of(((y + k) & (NY - 1)) * size, size), size)
        out_refs[k][...] = terms[rows, :]


def plane_kernel(coord_ref, _, keep_ref, *refs):
    in_refs, out_refs, total = refs[:3], refs[3:-1], refs[-1]
    z = coord_ref[3]
    value = keep_ref[...]
    for ref in in_refs:
        value = value + ref[...].astype(F32)
    total[...] = value
    for k in range(NZ):
        rows = pl.ds(pl.multiple_of(((z + k) & (NZ - 1)) * ROWS, ROWS), ROWS)
        out_refs[k][...] = total[rows, :].astype(out_refs[k].dtype)


def swap(values):
    return lax.ppermute(values, "c", [(0, 1), (1, 0)])


def shift(values, axis, size, step):
    return lax.ppermute(values, axis, [(i, (i + step) % size) for i in range(size)])


def exchange(values, axes):
    return lax.all_to_all(values, axes, 0, 0, tiled=True)


def gather(values, axes, size):
    return exchange(jnp.broadcast_to(values[None], (size,) + values.shape), axes)


def pick(values, place):
    return lax.dynamic_index_in_dim(values, place, 0, keepdims=False)


def count(coord, token, received, *counted):
    return pl.pallas_call(
        functools.partial(count_kernel, not counted),
        out_shape=[jax.ShapeDtypeStruct((2, NY * NC * ROWS, NZ * ROWS), F32), TOKEN],
        in_specs=[SMEM, ANY, VMEM] + [VMEM] * len(counted),
        out_specs=[VMEM, VMEM],
        scratch_shapes=[
            pltpu.VMEM((NDEV, CAP), I32),
            pltpu.VMEM((NDEV, CAP), I32),
            pltpu.VMEM((NDEV, CAP), F32),
        ],
        compiler_params=params(),
        cost_estimate=pl.CostEstimate(flops=12_000_000_000, bytes_accessed=2_400_000, transcendentals=0),
        name="count",
    )(coord, token, received, *counted)


def per_device(node_aggregate, weight, tiles, tile_src, tile_dst, tile_count, pair_owner, pair_row):
    pair_total = pair_owner.shape[0]
    slots = tiles.shape[0]
    c = lax.axis_index("c")
    coord = jnp.stack(
        [lax.axis_index("y"), c, lax.axis_index("x"), lax.axis_index("z")]
    ).astype(I32)

    with jax.named_scope("hidden"):
        pre_act = jnp.dot(node_aggregate, weight, preferred_element_type=F32)
        hidden, act_back = jax.vjp(activation, pre_act)
        hidden_b = hidden.astype(BF)

    with jax.named_scope("pair_exchange"):
        ring = gather(hidden_b, "z", NZ).reshape(NZ * ROWS, F)
        ends, token = pl.pallas_call(
            bucket_kernel,
            out_shape=[jax.ShapeDtypeStruct((NDEV, 4 * CAP), BF), TOKEN],
            in_specs=[VMEM, VMEM],
            out_specs=[VMEM, VMEM],
            scratch_shapes=[pltpu.VMEM((4 * NDEV, CAP), F32)],
            compiler_params=params(),
            cost_estimate=pl.CostEstimate(flops=9_000_000_000, bytes_accessed=400_000, transcendentals=0),
            name="bucket",
        )(pair_owner.T, pair_row.T)
        ends = ends.reshape(NDEV, 2, 2 * CAP)
        ring, ends = lax.optimization_barrier((ring, ends))
        planes = [ring] + [shift(ring, "y", NY, -k) for k in range(1, NY)]
        received = exchange(ends, ("y", "z", "c")).reshape(NDEV, 4 * CAP)
        counted, token = count(coord, token, received)
        columns = node_aggregate.reshape(ROWS, NX * NC, ROWS).transpose(1, 0, 2)
        planes, columns, token = lax.optimization_barrier((planes, columns, token))
        planes = planes + [swap(plane) for plane in planes]
        counted, _ = count(coord, token, received, counted)

    with jax.named_scope("tile_matrix"):
        halves = tiles.reshape(slots, 2, ROWS, tiles.shape[2]).transpose(1, 0, 2, 3)
        own_half = pick(halves, c)
        other_half = swap(pick(halves, 1 - c))
        meta = jnp.concatenate([tile_src, tile_dst, tile_count]).astype(I32)
        metas = jnp.stack([meta, swap(meta)])
        high, low, token = pl.pallas_call(
            tiles_kernel,
            out_shape=[jax.ShapeDtypeStruct((NY * NZ * ROWS, 512), BF)] * 2 + [TOKEN],
            in_specs=[SMEM, VMEM, VMEM],
            out_specs=[VMEM] * 3,
            scratch_shapes=[pltpu.VMEM((NY * NZ * ROWS, 512), F32)],
            compiler_params=params(),
            cost_estimate=pl.CostEstimate(flops=3_000_000_000, bytes_accessed=5_000_000, transcendentals=0),
            name="tile_sum",
        )(metas, own_half, other_half)
        nodes = exchange(columns, ("x", "c"))

    with jax.named_scope("hidden_grad"):
        own, token, nodes = lax.optimization_barrier((hidden_b, token, nodes))
        hidden_grad = pl.pallas_call(
            functools.partial(grad_kernel, ROWS / (2.0 * pair_total)),
            out_shape=jax.ShapeDtypeStruct((ROWS, F), F32),
            in_specs=[ANY] + [VMEM] * (2 + len(planes)),
            out_specs=VMEM,
            compiler_params=params(),
            cost_estimate=pl.CostEstimate(flops=5_000_000_000, bytes_accessed=6_000_000, transcendentals=262144),
            name="pair_grad",
        )(token, own, counted, *planes)
        pre_grad = act_back(hidden_grad)[0].astype(BF)

    with jax.named_scope("spread"):
        pre_parts = []
        for dc in range(NC):
            for dx in range(NX):
                pairs = [
                    (((x + dx) % NX) * NC + (b ^ dc), x * NC + b) for x in range(NX) for b in range(NC)
                ]
                away = dc + dx > 0
                pre_parts.append(lax.ppermute(pre_grad, ("x", "c"), pairs) if away else pre_grad)
        *terms, token = pl.pallas_call(
            terms_kernel,
            out_shape=[jax.ShapeDtypeStruct((ROWS // NY, F), F32)] * NY + [TOKEN],
            in_specs=[SMEM] + [VMEM] * 9,
            out_specs=[VMEM] * (NY + 1),
            scratch_shapes=[pltpu.VMEM((ROWS, F), F32)],
            compiler_params=params(),
            cost_estimate=pl.CostEstimate(flops=1_000_000_000, bytes_accessed=700_000, transcendentals=0),
            name="weight_terms",
        )(coord, nodes, *pre_parts)
        keep, *send, token = pl.pallas_call(
            spread_kernel,
            out_shape=[
                jax.ShapeDtypeStruct((NZ * ROWS, F), dtype) for dtype in (F32,) + (BF,) * (NY - 1)
            ]
            + [TOKEN],
            in_specs=[SMEM, ANY] + [VMEM] * 11,
            out_specs=[VMEM] * (NY + 1),
            scratch_shapes=[pltpu.VMEM((NC * NX * ROWS, F), BF)],
            compiler_params=params(),
            cost_estimate=pl.CostEstimate(flops=5_000_000_000, bytes_accessed=8_000_000, transcendentals=0),
            name="spread",
        )(coord, token, weight, high, low, *pre_parts)

    with jax.named_scope("sums"):
        planes = [shift(send[k - 1], "y", NY, k) for k in (2, 1, 3)]
        others = [shift(terms[k], "y", NY, k) for k in range(1, NY)]
        *others, token = lax.optimization_barrier((*others, token))
        share = terms[0]
        for other in others:
            share = share + other
        shares = gather(share, "z", NZ)
        block = shares[0]
        for k in range(1, NZ):
            block = block + shares[k]
        own, *parts = pl.pallas_call(
            plane_kernel,
            out_shape=[
                jax.ShapeDtypeStruct((ROWS, F), dtype) for dtype in (F32,) + (BF,) * (NZ - 1)
            ],
            in_specs=[SMEM, ANY] + [VMEM] * 4,
            out_specs=[VMEM] * NZ,
            scratch_shapes=[pltpu.VMEM((NZ * ROWS, F), F32)],
            compiler_params=params(),
            cost_estimate=pl.CostEstimate(flops=2_000_000_000, bytes_accessed=3_000_000, transcendentals=0),
            name="plane_sum",
        )(coord, token, keep, *planes)
        own, block = lax.optimization_barrier((own, block))
        feature = own
        for k in (4, 3, 5, 2, 6, 1, 7):
            feature = feature + shift(parts[k - 1], "z", NZ, k).astype(F32)
        feature_grad = feature.astype(BF)
        weight_grad = gather(block, ("x", "c", "y"), NX * NC * NY).reshape(F, F)
    return (feature_grad, weight_grad)


def solution(mesh):
    grid = Mesh(mesh.devices.reshape(NX, NY, NZ, NC), ("x", "y", "z", "c"))
    split = P(("x", "y", "z", "c"))
    return jax.shard_map(
        per_device,
        mesh=grid,
        in_specs=(split, P(), split, split, split, split, split, split),
        out_specs=(split, P()),
        check_vma=False,
    )
```

```python
import functools
import math

import jax
import jax.numpy as jnp
from jax import lax
from jax.experimental import pallas as pl
from jax.experimental.pallas import tpu as pltpu
from jax.sharding import Mesh, PartitionSpec as P

NX, NY, NZ, NC = 4, 4, 8, 2
NDEV = NY * NZ * NC
ROWS = 64
F = 512
CAP = 512
BF = jnp.bfloat16
F32 = jnp.float32
I32 = jnp.int32
POS = 4096.0
SUB = 256
SUBS = 8
NT = (((1,), (1,)), ((), ()))
TN = (((0,), (0,)), ((), ()))
VMEM = pl.BlockSpec(memory_space=pltpu.VMEM)
SMEM = pl.BlockSpec(memory_space=pltpu.SMEM)
ANY = pl.BlockSpec(memory_space=pl.ANY)


TOKEN = jax.ShapeDtypeStruct((8, 128), F32)


def params(mib=16):
    return pltpu.CompilerParams(vmem_limit_bytes=mib << 20)


def activation(values):
    return jax.nn.gelu(values)


def bucket_kernel(owner_ref, row_ref, out_ref, token_ref, acc):
    token_ref[...] = jnp.zeros_like(token_ref)
    total = owner_ref.shape[1]
    positives = total // 5
    step = SUB * SUBS
    tri = (
        lax.broadcasted_iota(I32, (SUB, SUB), 0) < lax.broadcasted_iota(I32, (SUB, SUB), 1)
    ).astype(BF)
    acc[...] = jnp.zeros_like(acc)
    base = jnp.zeros((NDEV, 1), F32)
    for end in range(2):

        def body(j, base, end=end):
            ranks, parts = [], [[], [], [], []]
            for s in range(SUBS):
                start = pl.multiple_of(j * step + s * SUB, SUB)
                here = pl.ds(start, SUB)
                own = owner_ref[end : end + 1, here]
                same = lax.broadcasted_iota(I32, (NDEV, SUB), 0) == own
                hot = same.astype(F32)
                prefix = jnp.dot(hot.astype(BF), tri, preferred_element_type=F32)
                ranks.append(jnp.sum(hot * (prefix + base), axis=0, keepdims=True))
                base = base + jnp.sum(hot, axis=1, keepdims=True)
                place = start + lax.broadcasted_iota(I32, (1, SUB), 1)
                weight = jnp.where(place < positives, POS, 1.0)
                values = [
                    weight,
                    row_ref[end : end + 1, here].astype(F32),
                    owner_ref[1 - end : 2 - end, here].astype(F32),
                    row_ref[1 - end : 2 - end, here].astype(F32),
                ]
                for v in range(4):
                    parts[v].append((hot * values[v]).astype(BF))
            left = jnp.concatenate([jnp.concatenate(p, axis=1) for p in parts], axis=0)
            rank = jnp.concatenate(ranks, axis=1).astype(I32)
            right = (lax.broadcasted_iota(I32, (CAP, step), 0) == rank).astype(F32).astype(BF)
            acc[...] += lax.dot_general(left, right, NT, preferred_element_type=F32)
            return base

        base = lax.fori_loop(0, total // step, body, base)
    for v in range(4):
        out_ref[:, v * CAP : (v + 1) * CAP] = acc[v * NDEV : (v + 1) * NDEV, :].astype(BF)


def count_kernel(coord_ref, recv_ref, near_ref, far_ref, token_ref, left_at, right_at, weight_at):
    token_ref[...] = jnp.zeros_like(token_ref)
    y, c = coord_ref[0], coord_ref[1]
    weight_at[...] = recv_ref[:, 0:CAP].astype(F32)
    own_row = recv_ref[:, CAP : 2 * CAP].astype(F32).astype(I32)
    owner = recv_ref[:, 2 * CAP : 3 * CAP].astype(F32).astype(I32)
    row = recv_ref[:, 3 * CAP : 4 * CAP].astype(F32).astype(I32)
    piece = ((owner & 1) ^ c) * NY + (((owner >> 4) - y) & (NY - 1))
    left_at[...] = piece * ROWS + own_row
    right_at[...] = ((owner >> 1) & (NZ - 1)) * ROWS + row
    near_ref[...] = jnp.zeros_like(near_ref)
    far_ref[...] = jnp.zeros_like(far_ref)
    group = 7
    groups = NDEV // group
    size = NY * ROWS

    def add(start, count):
        spots = lax.broadcasted_iota(I32, (CAP, CAP), 0)
        left, right = [], []
        for s in range(count):
            here = pl.ds(start + s, 1)
            left.append(jnp.where(spots == left_at[here, :], weight_at[here, :], 0.0).astype(BF))
            right.append(jnp.where(spots == right_at[here, :], 1.0, 0.0).astype(BF))
        total = lax.dot_general(
            jnp.concatenate(left, axis=1), jnp.concatenate(right, axis=1), NT, preferred_element_type=F32
        )
        ones = jnp.floor(total * (1.0 / POS))
        both = total - (POS - 1.0) * ones
        near_ref[0] += both[:size]
        near_ref[1] += ones[:size]
        far_ref[0] += both[size:]
        far_ref[1] += ones[size:]

    def body(g, carry):
        add(g * group, group)
        return carry

    lax.fori_loop(0, groups, body, 0)
    add(groups * group, NDEV - groups * group)


def grad_kernel(scale, _, own_ref, count_ref, *refs):
    pieces, rest, out_ref = refs[:NY], refs[NY:-1], refs[-1]
    own = own_ref[...]
    total = rest[0][...] if rest else jnp.zeros((ROWS, F), F32)
    for k in range(NY):
        nodes = pieces[k][...]
        score = lax.dot_general(own, nodes, NT, preferred_element_type=F32) / math.sqrt(F)
        here = slice(k * ROWS, (k + 1) * ROWS)
        grad = (count_ref[0, here, :] * jax.nn.sigmoid(score) - count_ref[1, here, :]) * scale
        high = grad.astype(BF)
        low = (grad - high.astype(F32)).astype(BF)
        total += jnp.dot(high, nodes, preferred_element_type=F32)
        total += jnp.dot(low, nodes, preferred_element_type=F32)
    out_ref[...] = total


def tiles_kernel(meta_ref, own_ref, other_ref, high_ref, low_ref, token_ref, acc):
    token_ref[...] = jnp.zeros_like(token_ref)
    slots = own_ref.shape[0]
    acc[...] = jnp.zeros_like(acc)
    for part, tiles_ref in enumerate((own_ref, other_ref)):

        def body(s, carry, part=part, tiles_ref=tiles_ref):
            rows = pl.ds(pl.multiple_of(meta_ref[part, s] * ROWS, ROWS), ROWS)
            dst = meta_ref[part, slots + s]
            columns = pl.ds(pl.multiple_of(part * 256 + dst * 128, 128), 128)
            acc[rows, columns] += tiles_ref[s].astype(F32)
            return carry

        lax.fori_loop(0, meta_ref[part, 2 * slots], body, 0)

    def split(k, carry):
        rows = pl.ds(pl.multiple_of(k * 128, 128), 128)
        value = acc[rows, :]
        high = value.astype(BF)
        high_ref[rows, :] = high
        low_ref[rows, :] = (value - high.astype(F32)).astype(BF)
        return carry

    lax.fori_loop(0, acc.shape[0] // 128, split, 0)


def spread_kernel(coord_ref, _, weight_ref, high_ref, low_ref, *refs):
    pre_refs, out_ref, token_ref, pre = refs[:NC], refs[NC], refs[-2], refs[-1]
    token_ref[...] = jnp.zeros_like(token_ref)
    x = coord_ref[2]
    for k in range(NC * NX):
        dc, dx = k // NX, k % NX
        place = pl.multiple_of((dc * NX + ((x + dx) & (NX - 1))) * ROWS, ROWS)
        pre[pl.ds(place, ROWS), :] = pre_refs[dc][dx * ROWS : (dx + 1) * ROWS, :]
    agg = lax.dot_general(pre[...], weight_ref[...], NT, preferred_element_type=F32).astype(BF)
    size = NZ * ROWS
    for k in range(NY):
        rows = slice(k * size, (k + 1) * size)
        part = jnp.dot(high_ref[rows, :], agg, preferred_element_type=F32)
        part += jnp.dot(low_ref[rows, :], agg, preferred_element_type=F32)
        out_ref[k] = part.astype(BF)


def terms_kernel(coord_ref, node_ref, *refs):
    pre_refs, out_refs, token_ref, terms = refs[:NC], refs[NC:-2], refs[-2], refs[-1]
    token_ref[...] = jnp.zeros_like(token_ref)
    y, c, x = coord_ref[0], coord_ref[1], coord_ref[2]
    total = jnp.zeros(terms.shape, F32)
    for k in range(NC * NX):
        dc, dx = k // NX, k % NX
        node = node_ref[((x + dx) & (NX - 1)) * NC + (c ^ dc)]
        pre = pre_refs[dc][dx * ROWS : (dx + 1) * ROWS, :]
        total += lax.dot_general(node, pre, TN, preferred_element_type=F32)
    terms[...] = total
    size = ROWS // NY
    for k in range(NY):
        rows = pl.ds(pl.multiple_of(((y + k) & (NY - 1)) * size, size), size)
        out_refs[k][...] = terms[rows, :]


def plane_kernel(coord_ref, _, in_ref, *refs):
    out_refs, total = refs[:-1], refs[-1]
    z = coord_ref[3]
    value = in_ref[0].astype(F32)
    for k in range(1, NY):
        value = value + in_ref[k].astype(F32)
    total[...] = value
    for k in range(NZ):
        rows = pl.ds(pl.multiple_of(((z + k) & (NZ - 1)) * ROWS, ROWS), ROWS)
        out_refs[k][...] = total[rows, :].astype(out_refs[k].dtype)


def share_kernel(coord_ref, *refs):
    in_refs, out_ref, token_ref, parts = refs[:NZ], refs[NZ], refs[NZ + 1], refs[-1]
    token_ref[...] = jnp.zeros_like(token_ref)
    z = coord_ref[3]
    for k in range(NZ):
        parts[(z + k) & (NZ - 1)] = in_refs[k][...]
    value = parts[0]
    for k in range(1, NZ):
        value = value + parts[k]
    out_ref[...] = value


def swap(values):
    return lax.ppermute(values, "c", [(0, 1), (1, 0)])


def shift(values, axis, size, step):
    return lax.ppermute(values, axis, [(i, (i + step) % size) for i in range(size)])


def exchange(values, axes):
    return lax.all_to_all(values, axes, 0, 0, tiled=True)


def gather(values, axes, size):
    return exchange(jnp.broadcast_to(values[None], (size,) + values.shape), axes)


def pick(values, place):
    return lax.dynamic_index_in_dim(values, place, 0, keepdims=False)


def count(coord, received):
    half = jax.ShapeDtypeStruct((2, NY * ROWS, NZ * ROWS), F32)
    return pl.pallas_call(
        count_kernel,
        out_shape=[half, half, TOKEN],
        in_specs=[SMEM, VMEM],
        out_specs=[VMEM] * 3,
        scratch_shapes=[
            pltpu.VMEM((NDEV, CAP), I32),
            pltpu.VMEM((NDEV, CAP), I32),
            pltpu.VMEM((NDEV, CAP), F32),
        ],
        compiler_params=params(),
        cost_estimate=pl.CostEstimate(flops=24_000_000_000, bytes_accessed=2_400_000, transcendentals=0),
        name="count",
    )(coord, received)


def pair_grad(scale, token, own, counted, *arrays):
    return pl.pallas_call(
        functools.partial(grad_kernel, scale),
        out_shape=jax.ShapeDtypeStruct((ROWS, F), F32),
        in_specs=[ANY] + [VMEM] * (2 + len(arrays)),
        out_specs=VMEM,
        compiler_params=params(),
        cost_estimate=pl.CostEstimate(flops=3_000_000_000, bytes_accessed=3_000_000, transcendentals=131072),
        name="pair_grad",
    )(token, own, counted, *arrays)


def per_device(node_aggregate, weight, tiles, tile_src, tile_dst, tile_count, pair_owner, pair_row):
    pair_total = pair_owner.shape[0]
    slots = tiles.shape[0]
    c = lax.axis_index("c")
    coord = jnp.stack(
        [lax.axis_index("y"), c, lax.axis_index("x"), lax.axis_index("z")]
    ).astype(I32)

    with jax.named_scope("hidden"):
        pre_act = jnp.dot(node_aggregate, weight, preferred_element_type=F32)
        hidden, act_back = jax.vjp(activation, pre_act)
        hidden_b = hidden.astype(BF)

    with jax.named_scope("pair_exchange"):
        ring = gather(hidden_b, "z", NZ).reshape(NZ * ROWS, F)
        ends, token = pl.pallas_call(
            bucket_kernel,
            out_shape=[jax.ShapeDtypeStruct((NDEV, 4 * CAP), BF), TOKEN],
            in_specs=[VMEM, VMEM],
            out_specs=[VMEM, VMEM],
            scratch_shapes=[pltpu.VMEM((4 * NDEV, CAP), F32)],
            compiler_params=params(),
            cost_estimate=pl.CostEstimate(flops=9_000_000_000, bytes_accessed=400_000, transcendentals=0),
            name="bucket",
        )(pair_owner.T, pair_row.T)
        ends = ends.reshape(NDEV, 2, 2 * CAP)
        ring, ends = lax.optimization_barrier((ring, ends))
        planes = [ring] + [shift(ring, "y", NY, -k) for k in range(1, NY)]
        received = exchange(ends, ("y", "z", "c")).reshape(NDEV, 4 * CAP)
        near, far, token = count(coord, received)

    with jax.named_scope("tile_matrix"):
        halves = tiles.reshape(slots, 2, ROWS, tiles.shape[2]).transpose(1, 0, 2, 3)
        own_half = pick(halves, c)
        other_half = swap(pick(halves, 1 - c))
        meta = jnp.concatenate([tile_src, tile_dst, tile_count]).astype(I32)
        metas = jnp.stack([meta, swap(meta)])
        columns = node_aggregate.reshape(ROWS, NX * NC, ROWS).transpose(1, 0, 2)
        far_ring = swap(ring)
        *planes, columns, metas, token = lax.optimization_barrier((*planes, columns, metas, token))
        far_planes = [far_ring] + [swap(plane) for plane in planes[1:]]
        high, low, tile_token = pl.pallas_call(
            tiles_kernel,
            out_shape=[jax.ShapeDtypeStruct((NY * NZ * ROWS, 512), BF)] * 2 + [TOKEN],
            in_specs=[SMEM, VMEM, VMEM],
            out_specs=[VMEM] * 3,
            scratch_shapes=[pltpu.VMEM((NY * NZ * ROWS, 512), F32)],
            compiler_params=params(),
            cost_estimate=pl.CostEstimate(flops=3_000_000_000, bytes_accessed=5_000_000, transcendentals=0),
            name="tile_sum",
        )(metas, own_half, other_half)
        nodes = exchange(columns, ("x", "c"))

    with jax.named_scope("hidden_grad"):
        scale = ROWS / (2.0 * pair_total)
        hidden_grad = pair_grad(scale, token, hidden_b, near, *planes)
        own, tile_token, nodes = lax.optimization_barrier((hidden_b, tile_token, nodes))
        hidden_grad = pair_grad(scale, tile_token, own, far, *far_planes, hidden_grad)
        pre_grad = act_back(hidden_grad)[0].astype(BF)

    with jax.named_scope("spread"):
        along_x = [pre_grad] + [shift(pre_grad, "x", NX, -k) for k in range(1, NX)]
        near_pre = jnp.concatenate(along_x, axis=0)
        pre_parts = [near_pre, swap(near_pre)]
        *terms, token = pl.pallas_call(
            terms_kernel,
            out_shape=[jax.ShapeDtypeStruct((ROWS // NY, F), F32)] * NY + [TOKEN],
            in_specs=[SMEM] + [VMEM] * 3,
            out_specs=[VMEM] * (NY + 1),
            scratch_shapes=[pltpu.VMEM((ROWS, F), F32)],
            compiler_params=params(),
            cost_estimate=pl.CostEstimate(flops=1_000_000_000, bytes_accessed=700_000, transcendentals=0),
            name="weight_terms",
        )(coord, nodes, *pre_parts)
        send, token = pl.pallas_call(
            spread_kernel,
            out_shape=[jax.ShapeDtypeStruct((NY, NZ * ROWS, F), BF), TOKEN],
            in_specs=[SMEM, ANY] + [VMEM] * 5,
            out_specs=[VMEM] * 2,
            scratch_shapes=[pltpu.VMEM((NC * NX * ROWS, F), BF)],
            compiler_params=params(),
            cost_estimate=pl.CostEstimate(flops=5_000_000_000, bytes_accessed=8_000_000, transcendentals=0),
            name="spread",
        )(coord, token, weight, high, low, *pre_parts)

    with jax.named_scope("sums"):
        planes = exchange(send, "y")
        *terms, token = lax.optimization_barrier((*terms, token))
        share = terms[0]
        for k in range(1, NY):
            share = share + shift(terms[k], "y", NY, k)
        block, share_token = pl.pallas_call(
            share_kernel,
            out_shape=[jax.ShapeDtypeStruct((ROWS // NY, F), F32), TOKEN],
            in_specs=[SMEM] + [VMEM] * NZ,
            out_specs=[VMEM] * 2,
            scratch_shapes=[pltpu.VMEM((NZ, ROWS // NY, F), F32)],
            compiler_params=params(),
            cost_estimate=pl.CostEstimate(flops=1_000_000, bytes_accessed=300_000, transcendentals=0),
            name="share_sum",
        )(coord, share, *[shift(share, "z", NZ, -k) for k in range(1, NZ)])
        token, share_token = lax.optimization_barrier((token, share_token))
        own, *parts = pl.pallas_call(
            plane_kernel,
            out_shape=[
                jax.ShapeDtypeStruct((ROWS, F), dtype) for dtype in (F32,) + (BF,) * (NZ - 1)
            ],
            in_specs=[SMEM, ANY, VMEM],
            out_specs=[VMEM] * NZ,
            scratch_shapes=[pltpu.VMEM((NZ * ROWS, F), F32)],
            compiler_params=params(),
            cost_estimate=pl.CostEstimate(flops=2_000_000_000, bytes_accessed=3_000_000, transcendentals=0),
            name="plane_sum",
        )(coord, share_token, planes)
        feature = own
        for k in (1, 7, 4, 2, 6, 3, 5):
            feature = feature + shift(parts[k - 1], "z", NZ, k).astype(F32)
        feature_grad = feature.astype(BF)
        weight_grad = gather(block, ("x", "c", "y"), NX * NC * NY).reshape(F, F)
    return (feature_grad, weight_grad)


def solution(mesh):
    grid = Mesh(mesh.devices.reshape(NX, NY, NZ, NC), ("x", "y", "z", "c"))
    split = P(("x", "y", "z", "c"))
    return jax.shard_map(
        per_device,
        mesh=grid,
        in_specs=(split, P(), split, split, split, split, split, split),
        out_specs=(split, P()),
        check_vma=False,
    )
```

```python
import functools
import math

import jax
import jax.numpy as jnp
from jax import lax
from jax.experimental import pallas as pl
from jax.experimental.pallas import tpu as pltpu
from jax.sharding import Mesh, PartitionSpec as P

NX, NY, NZ, NC = 4, 4, 8, 2
NDEV = NY * NZ * NC
ROWS = 64
F = 512
CAP = 512
BF = jnp.bfloat16
F32 = jnp.float32
I32 = jnp.int32
POS = 4096.0
SUB = 256
SUBS = 8
NT = (((1,), (1,)), ((), ()))
TN = (((0,), (0,)), ((), ()))
VMEM = pl.BlockSpec(memory_space=pltpu.VMEM)
SMEM = pl.BlockSpec(memory_space=pltpu.SMEM)
ANY = pl.BlockSpec(memory_space=pl.ANY)


TOKEN = jax.ShapeDtypeStruct((8, 128), F32)


def params(mib=16):
    return pltpu.CompilerParams(vmem_limit_bytes=mib << 20)


def activation(values):
    return jax.nn.gelu(values)


def bucket_kernel(owner_ref, row_ref, out_ref, token_ref, acc):
    token_ref[...] = jnp.zeros_like(token_ref)
    total = owner_ref.shape[1]
    positives = total // 5
    step = SUB * SUBS
    tri = (
        lax.broadcasted_iota(I32, (SUB, SUB), 0) < lax.broadcasted_iota(I32, (SUB, SUB), 1)
    ).astype(BF)
    acc[...] = jnp.zeros_like(acc)
    base = jnp.zeros((NDEV, 1), F32)
    for end in range(2):

        def body(j, base, end=end):
            ranks, parts = [], [[], [], [], []]
            for s in range(SUBS):
                start = pl.multiple_of(j * step + s * SUB, SUB)
                here = pl.ds(start, SUB)
                own = owner_ref[end : end + 1, here]
                same = lax.broadcasted_iota(I32, (NDEV, SUB), 0) == own
                hot = same.astype(F32)
                prefix = jnp.dot(hot.astype(BF), tri, preferred_element_type=F32)
                ranks.append(jnp.sum(hot * (prefix + base), axis=0, keepdims=True))
                base = base + jnp.sum(hot, axis=1, keepdims=True)
                place = start + lax.broadcasted_iota(I32, (1, SUB), 1)
                weight = jnp.where(place < positives, POS, 1.0)
                values = [
                    weight,
                    row_ref[end : end + 1, here].astype(F32),
                    owner_ref[1 - end : 2 - end, here].astype(F32),
                    row_ref[1 - end : 2 - end, here].astype(F32),
                ]
                for v in range(4):
                    parts[v].append((hot * values[v]).astype(BF))
            left = jnp.concatenate([jnp.concatenate(p, axis=1) for p in parts], axis=0)
            rank = jnp.concatenate(ranks, axis=1).astype(I32)
            right = (lax.broadcasted_iota(I32, (CAP, step), 0) == rank).astype(F32).astype(BF)
            acc[...] += lax.dot_general(left, right, NT, preferred_element_type=F32)
            return base

        base = lax.fori_loop(0, total // step, body, base)
    for v in range(4):
        out_ref[:, v * CAP : (v + 1) * CAP] = acc[v * NDEV : (v + 1) * NDEV, :].astype(BF)


def count_kernel(coord_ref, recv_ref, near_ref, far_ref, token_ref, left_at, right_at, weight_at):
    token_ref[...] = jnp.zeros_like(token_ref)
    y, c = coord_ref[0], coord_ref[1]
    weight_at[...] = recv_ref[:, 0:CAP].astype(F32)
    own_row = recv_ref[:, CAP : 2 * CAP].astype(F32).astype(I32)
    owner = recv_ref[:, 2 * CAP : 3 * CAP].astype(F32).astype(I32)
    row = recv_ref[:, 3 * CAP : 4 * CAP].astype(F32).astype(I32)
    piece = ((owner & 1) ^ c) * NY + (((owner >> 4) - y) & (NY - 1))
    left_at[...] = piece * ROWS + own_row
    right_at[...] = ((owner >> 1) & (NZ - 1)) * ROWS + row
    near_ref[...] = jnp.zeros_like(near_ref)
    far_ref[...] = jnp.zeros_like(far_ref)
    group = 7
    groups = NDEV // group
    size = NY * ROWS

    def add(start, count):
        spots = lax.broadcasted_iota(I32, (CAP, CAP), 0)
        left, right = [], []
        for s in range(count):
            here = pl.ds(start + s, 1)
            left.append(jnp.where(spots == left_at[here, :], weight_at[here, :], 0.0).astype(BF))
            right.append(jnp.where(spots == right_at[here, :], 1.0, 0.0).astype(BF))
        total = lax.dot_general(
            jnp.concatenate(left, axis=1), jnp.concatenate(right, axis=1), NT, preferred_element_type=F32
        )
        ones = jnp.floor(total * (1.0 / POS))
        both = total - (POS - 1.0) * ones
        near_ref[0] += both[:size]
        near_ref[1] += ones[:size]
        far_ref[0] += both[size:]
        far_ref[1] += ones[size:]

    def body(g, carry):
        add(g * group, group)
        return carry

    lax.fori_loop(0, groups, body, 0)
    add(groups * group, NDEV - groups * group)


def grad_kernel(scale, _, own_ref, count_ref, *refs):
    pieces, rest, out_ref = refs[:NY], refs[NY:-1], refs[-1]
    own = own_ref[...]
    total = rest[0][...] if rest else jnp.zeros((ROWS, F), F32)
    for k in range(NY):
        nodes = pieces[k][...]
        score = lax.dot_general(own, nodes, NT, preferred_element_type=F32) / math.sqrt(F)
        here = slice(k * ROWS, (k + 1) * ROWS)
        grad = (count_ref[0, here, :] * jax.nn.sigmoid(score) - count_ref[1, here, :]) * scale
        high = grad.astype(BF)
        low = (grad - high.astype(F32)).astype(BF)
        total += jnp.dot(high, nodes, preferred_element_type=F32)
        total += jnp.dot(low, nodes, preferred_element_type=F32)
    out_ref[...] = total


def tiles_kernel(meta_ref, own_ref, other_ref, high_ref, low_ref, acc):
    slots = own_ref.shape[0]
    acc[...] = jnp.zeros_like(acc)
    for part, tiles_ref in enumerate((own_ref, other_ref)):

        def body(s, carry, part=part, tiles_ref=tiles_ref):
            rows = pl.ds(pl.multiple_of(meta_ref[part, s] * ROWS, ROWS), ROWS)
            dst = meta_ref[part, slots + s]
            columns = pl.ds(pl.multiple_of(part * 256 + dst * 128, 128), 128)
            acc[rows, columns] += tiles_ref[s].astype(F32)
            return carry

        lax.fori_loop(0, meta_ref[part, 2 * slots], body, 0)

    def split(k, carry):
        rows = pl.ds(pl.multiple_of(k * 128, 128), 128)
        value = acc[rows, :]
        high = value.astype(BF)
        high_ref[rows, :] = high
        low_ref[rows, :] = (value - high.astype(F32)).astype(BF)
        return carry

    lax.fori_loop(0, acc.shape[0] // 128, split, 0)


def spread_kernel(coord_ref, _, weight_ref, high_ref, low_ref, *refs):
    pre_refs, out_ref, token_ref, pre = refs[:NC], refs[NC], refs[-2], refs[-1]
    token_ref[...] = jnp.zeros_like(token_ref)
    x = coord_ref[2]
    for k in range(NC * NX):
        dc, dx = k // NX, k % NX
        place = pl.multiple_of((dc * NX + ((x + dx) & (NX - 1))) * ROWS, ROWS)
        pre[pl.ds(place, ROWS), :] = pre_refs[dc][dx * ROWS : (dx + 1) * ROWS, :]
    agg = lax.dot_general(pre[...], weight_ref[...], NT, preferred_element_type=F32).astype(BF)
    size = NZ * ROWS
    for k in range(NY):
        rows = slice(k * size, (k + 1) * size)
        part = jnp.dot(high_ref[rows, :], agg, preferred_element_type=F32)
        part += jnp.dot(low_ref[rows, :], agg, preferred_element_type=F32)
        out_ref[k] = part.astype(BF)


def terms_kernel(coord_ref, node_ref, *refs):
    pre_refs, out_refs, token_ref, terms = refs[:NC], refs[NC:-2], refs[-2], refs[-1]
    token_ref[...] = jnp.zeros_like(token_ref)
    y = coord_ref[0]
    half = NX * ROWS
    total = lax.dot_general(node_ref[:half, :], pre_refs[0][...], TN, preferred_element_type=F32)
    total += lax.dot_general(node_ref[half:, :], pre_refs[1][...], TN, preferred_element_type=F32)
    terms[...] = total
    size = ROWS // NY
    for k in range(NY):
        rows = pl.ds(pl.multiple_of(((y + k) & (NY - 1)) * size, size), size)
        out_refs[k][...] = terms[rows, :]


def plane_kernel(coord_ref, _, in_ref, *refs):
    out_refs, total = refs[:-1], refs[-1]
    z = coord_ref[3]
    value = in_ref[0].astype(F32)
    for k in range(1, NY):
        value = value + in_ref[k].astype(F32)
    total[...] = value
    for k in range(NZ):
        rows = pl.ds(pl.multiple_of(((z + k) & (NZ - 1)) * ROWS, ROWS), ROWS)
        out_refs[k][...] = total[rows, :].astype(out_refs[k].dtype)


def share_kernel(coord_ref, *refs):
    in_refs, out_ref, token_ref, parts = refs[:NZ], refs[NZ], refs[NZ + 1], refs[-1]
    token_ref[...] = jnp.zeros_like(token_ref)
    z = coord_ref[3]
    for k in range(NZ):
        parts[(z + k) & (NZ - 1)] = in_refs[k][...]
    value = parts[0]
    for k in range(1, NZ):
        value = value + parts[k]
    out_ref[...] = value


def swap(values):
    return lax.ppermute(values, "c", [(0, 1), (1, 0)])


def shift(values, axis, size, step):
    return lax.ppermute(values, axis, [(i, (i + step) % size) for i in range(size)])


def exchange(values, axes):
    return lax.all_to_all(values, axes, 0, 0, tiled=True)


def gather(values, axes, size):
    return exchange(jnp.broadcast_to(values[None], (size,) + values.shape), axes)


def pick(values, place):
    return lax.dynamic_index_in_dim(values, place, 0, keepdims=False)


def count(coord, received):
    half = jax.ShapeDtypeStruct((2, NY * ROWS, NZ * ROWS), F32)
    return pl.pallas_call(
        count_kernel,
        out_shape=[half, half, TOKEN],
        in_specs=[SMEM, VMEM],
        out_specs=[VMEM] * 3,
        scratch_shapes=[
            pltpu.VMEM((NDEV, CAP), I32),
            pltpu.VMEM((NDEV, CAP), I32),
            pltpu.VMEM((NDEV, CAP), F32),
        ],
        compiler_params=params(),
        cost_estimate=pl.CostEstimate(flops=24_000_000_000, bytes_accessed=2_400_000, transcendentals=0),
        name="count",
    )(coord, received)


def pair_grad(scale, token, own, counted, *arrays):
    return pl.pallas_call(
        functools.partial(grad_kernel, scale),
        out_shape=jax.ShapeDtypeStruct((ROWS, F), F32),
        in_specs=[ANY] + [VMEM] * (2 + len(arrays)),
        out_specs=VMEM,
        compiler_params=params(),
        cost_estimate=pl.CostEstimate(flops=3_000_000_000, bytes_accessed=3_000_000, transcendentals=131072),
        name="pair_grad",
    )(token, own, counted, *arrays)


def per_device(node_aggregate, weight, tiles, tile_src, tile_dst, tile_count, pair_owner, pair_row):
    pair_total = pair_owner.shape[0]
    slots = tiles.shape[0]
    c = lax.axis_index("c")
    coord = jnp.stack(
        [lax.axis_index("y"), c, lax.axis_index("x"), lax.axis_index("z")]
    ).astype(I32)

    with jax.named_scope("hidden"):
        pre_act = jnp.dot(node_aggregate, weight, preferred_element_type=F32)
        hidden, act_back = jax.vjp(activation, pre_act)
        hidden_b = hidden.astype(BF)

    with jax.named_scope("pair_exchange"):
        ring = gather(hidden_b, "z", NZ).reshape(NZ * ROWS, F)
        ends, token = pl.pallas_call(
            bucket_kernel,
            out_shape=[jax.ShapeDtypeStruct((NDEV, 4 * CAP), BF), TOKEN],
            in_specs=[VMEM, VMEM],
            out_specs=[VMEM, VMEM],
            scratch_shapes=[pltpu.VMEM((4 * NDEV, CAP), F32)],
            compiler_params=params(),
            cost_estimate=pl.CostEstimate(flops=9_000_000_000, bytes_accessed=400_000, transcendentals=0),
            name="bucket",
        )(pair_owner.T, pair_row.T)
        ends = ends.reshape(NDEV, 2, 2 * CAP)
        near_nodes = jnp.concatenate(
            [node_aggregate] + [shift(node_aggregate, "x", NX, -k) for k in range(1, NX)], axis=0
        )
        nodes = jnp.concatenate([near_nodes, swap(near_nodes)], axis=0)
        column = (lax.axis_index("x") * NC + c) * ROWS
        nodes = lax.dynamic_slice_in_dim(nodes, column, ROWS, axis=1)
        ring, ends, nodes = lax.optimization_barrier((ring, ends, nodes))
        planes = [ring] + [shift(ring, "y", NY, -k) for k in range(1, NY)]
        received = exchange(ends, ("y", "z", "c")).reshape(NDEV, 4 * CAP)
        near, far, token = count(coord, received)

    with jax.named_scope("tile_matrix"):
        halves = tiles.reshape(slots, 2, ROWS, tiles.shape[2]).transpose(1, 0, 2, 3)
        own_half = pick(halves, c)
        other_half = swap(pick(halves, 1 - c))
        meta = jnp.concatenate([tile_src, tile_dst, tile_count]).astype(I32)
        metas = jnp.stack([meta, swap(meta)])
        far_ring = swap(ring)
        *planes, token = lax.optimization_barrier((*planes, token))
        far_planes = [far_ring] + [swap(plane) for plane in planes[1:]]
    with jax.named_scope("hidden_grad"):
        scale = ROWS / (2.0 * pair_total)
        hidden_grad = pair_grad(scale, token, hidden_b, near, *planes)
        hidden_grad = pair_grad(scale, token, hidden_b, far, *far_planes, hidden_grad)
        pre_grad = act_back(hidden_grad)[0].astype(BF)
        pre_grad, metas = lax.optimization_barrier((pre_grad, metas))

    with jax.named_scope("spread"):
        high, low = pl.pallas_call(
            tiles_kernel,
            out_shape=[jax.ShapeDtypeStruct((NY * NZ * ROWS, 512), BF)] * 2,
            in_specs=[SMEM, VMEM, VMEM],
            out_specs=[VMEM] * 2,
            scratch_shapes=[pltpu.VMEM((NY * NZ * ROWS, 512), F32)],
            compiler_params=params(),
            cost_estimate=pl.CostEstimate(flops=3_000_000_000, bytes_accessed=5_000_000, transcendentals=0),
            name="tile_sum",
        )(metas, own_half, other_half)
        along_x = [pre_grad] + [shift(pre_grad, "x", NX, -k) for k in range(1, NX)]
        near_pre = jnp.concatenate(along_x, axis=0)
        pre_parts = [near_pre, swap(near_pre)]
        *terms, token = pl.pallas_call(
            terms_kernel,
            out_shape=[jax.ShapeDtypeStruct((ROWS // NY, F), F32)] * NY + [TOKEN],
            in_specs=[SMEM] + [VMEM] * 3,
            out_specs=[VMEM] * (NY + 1),
            scratch_shapes=[pltpu.VMEM((ROWS, F), F32)],
            compiler_params=params(),
            cost_estimate=pl.CostEstimate(flops=1_000_000_000, bytes_accessed=700_000, transcendentals=0),
            name="weight_terms",
        )(coord, nodes, *pre_parts)
        others = [shift(terms[k], "y", NY, k) for k in range(1, NY)]
        send, token = pl.pallas_call(
            spread_kernel,
            out_shape=[jax.ShapeDtypeStruct((NY, NZ * ROWS, F), BF), TOKEN],
            in_specs=[SMEM, ANY] + [VMEM] * 5,
            out_specs=[VMEM] * 2,
            scratch_shapes=[pltpu.VMEM((NC * NX * ROWS, F), BF)],
            compiler_params=params(),
            cost_estimate=pl.CostEstimate(flops=5_000_000_000, bytes_accessed=8_000_000, transcendentals=0),
            name="spread",
        )(coord, token, weight, high, low, *pre_parts)

    with jax.named_scope("sums"):
        *others, send, token = lax.optimization_barrier((*others, send, token))
        planes = exchange(send, "y")
        share = terms[0]
        for other in others:
            share = share + other
        block, share_token = pl.pallas_call(
            share_kernel,
            out_shape=[jax.ShapeDtypeStruct((ROWS // NY, F), F32), TOKEN],
            in_specs=[SMEM] + [VMEM] * NZ,
            out_specs=[VMEM] * 2,
            scratch_shapes=[pltpu.VMEM((NZ, ROWS // NY, F), F32)],
            compiler_params=params(),
            cost_estimate=pl.CostEstimate(flops=1_000_000, bytes_accessed=300_000, transcendentals=0),
            name="share_sum",
        )(coord, share, *[shift(share, "z", NZ, -k) for k in range(1, NZ)])
        token, share_token = lax.optimization_barrier((token, share_token))
        own, *parts = pl.pallas_call(
            plane_kernel,
            out_shape=[
                jax.ShapeDtypeStruct((ROWS, F), dtype) for dtype in (F32,) + (BF,) * (NZ - 1)
            ],
            in_specs=[SMEM, ANY, VMEM],
            out_specs=[VMEM] * NZ,
            scratch_shapes=[pltpu.VMEM((NZ * ROWS, F), F32)],
            compiler_params=params(),
            cost_estimate=pl.CostEstimate(flops=2_000_000_000, bytes_accessed=3_000_000, transcendentals=0),
            name="plane_sum",
        )(coord, share_token, planes)
        feature = own
        for k in (1, 7, 4, 2, 6, 3, 5):
            feature = feature + shift(parts[k - 1], "z", NZ, k).astype(F32)
        feature_grad = feature.astype(BF)
        weight_grad = gather(block, ("x", "c", "y"), NX * NC * NY).reshape(F, F)
    return (feature_grad, weight_grad)


def solution(mesh):
    grid = Mesh(mesh.devices.reshape(NX, NY, NZ, NC), ("x", "y", "z", "c"))
    split = P(("x", "y", "z", "c"))
    return jax.shard_map(
        per_device,
        mesh=grid,
        in_specs=(split, P(), split, split, split, split, split, split),
        out_specs=(split, P()),
        check_vma=False,
    )
```

```python
import functools
import math

import jax
import jax.numpy as jnp
from jax import lax
from jax.experimental import pallas as pl
from jax.experimental.pallas import tpu as pltpu
from jax.sharding import Mesh, PartitionSpec as P

NX, NY, NZ, NC = 4, 4, 8, 2
NDEV = NY * NZ * NC
ROWS = 64
F = 512
CAP = 512
BF = jnp.bfloat16
F32 = jnp.float32
I32 = jnp.int32
POS = 4096.0
SUB = 256
SUBS = 8
NT = (((1,), (1,)), ((), ()))
TN = (((0,), (0,)), ((), ()))
VMEM = pl.BlockSpec(memory_space=pltpu.VMEM)
SMEM = pl.BlockSpec(memory_space=pltpu.SMEM)
ANY = pl.BlockSpec(memory_space=pl.ANY)


TOKEN = jax.ShapeDtypeStruct((8, 128), F32)


def params(mib=16):
    return pltpu.CompilerParams(vmem_limit_bytes=mib << 20)


def activation(values):
    return jax.nn.gelu(values)


def bucket_kernel(owner_ref, row_ref, out_ref, token_ref, acc):
    token_ref[...] = jnp.zeros_like(token_ref)
    total = owner_ref.shape[1]
    positives = total // 5
    step = SUB * SUBS
    tri = (
        lax.broadcasted_iota(I32, (SUB, SUB), 0) < lax.broadcasted_iota(I32, (SUB, SUB), 1)
    ).astype(BF)
    acc[...] = jnp.zeros_like(acc)
    base = jnp.zeros((NDEV, 1), F32)
    for end in range(2):

        def body(j, base, end=end):
            ranks, parts = [], [[], [], [], []]
            for s in range(SUBS):
                start = pl.multiple_of(j * step + s * SUB, SUB)
                here = pl.ds(start, SUB)
                own = owner_ref[end : end + 1, here]
                same = lax.broadcasted_iota(I32, (NDEV, SUB), 0) == own
                hot = same.astype(F32)
                prefix = jnp.dot(hot.astype(BF), tri, preferred_element_type=F32)
                ranks.append(jnp.sum(hot * (prefix + base), axis=0, keepdims=True))
                base = base + jnp.sum(hot, axis=1, keepdims=True)
                place = start + lax.broadcasted_iota(I32, (1, SUB), 1)
                weight = jnp.where(place < positives, POS, 1.0)
                values = [
                    weight,
                    row_ref[end : end + 1, here].astype(F32),
                    owner_ref[1 - end : 2 - end, here].astype(F32),
                    row_ref[1 - end : 2 - end, here].astype(F32),
                ]
                for v in range(4):
                    parts[v].append((hot * values[v]).astype(BF))
            left = jnp.concatenate([jnp.concatenate(p, axis=1) for p in parts], axis=0)
            rank = jnp.concatenate(ranks, axis=1).astype(I32)
            right = (lax.broadcasted_iota(I32, (CAP, step), 0) == rank).astype(F32).astype(BF)
            acc[...] += lax.dot_general(left, right, NT, preferred_element_type=F32)
            return base

        base = lax.fori_loop(0, total // step, body, base)
    for v in range(4):
        out_ref[:, v * CAP : (v + 1) * CAP] = acc[v * NDEV : (v + 1) * NDEV, :].astype(BF)


def count_kernel(coord_ref, recv_ref, near_ref, far_ref, token_ref, left_at, right_at, weight_at):
    token_ref[...] = jnp.zeros_like(token_ref)
    y, c = coord_ref[0], coord_ref[1]
    weight_at[...] = recv_ref[:, 0:CAP].astype(F32)
    own_row = recv_ref[:, CAP : 2 * CAP].astype(F32).astype(I32)
    owner = recv_ref[:, 2 * CAP : 3 * CAP].astype(F32).astype(I32)
    row = recv_ref[:, 3 * CAP : 4 * CAP].astype(F32).astype(I32)
    piece = ((owner & 1) ^ c) * NY + (((owner >> 4) - y) & (NY - 1))
    left_at[...] = piece * ROWS + own_row
    right_at[...] = ((owner >> 1) & (NZ - 1)) * ROWS + row
    near_ref[...] = jnp.zeros_like(near_ref)
    far_ref[...] = jnp.zeros_like(far_ref)
    group = 7
    groups = NDEV // group
    size = NY * ROWS

    def add(start, count):
        spots = lax.broadcasted_iota(I32, (CAP, CAP), 0)
        left, right = [], []
        for s in range(count):
            here = pl.ds(start + s, 1)
            left.append(jnp.where(spots == left_at[here, :], weight_at[here, :], 0.0).astype(BF))
            right.append(jnp.where(spots == right_at[here, :], 1.0, 0.0).astype(BF))
        total = lax.dot_general(
            jnp.concatenate(left, axis=1), jnp.concatenate(right, axis=1), NT, preferred_element_type=F32
        )
        ones = jnp.floor(total * (1.0 / POS))
        both = total - (POS - 1.0) * ones
        near_ref[0] += both[:size]
        near_ref[1] += ones[:size]
        far_ref[0] += both[size:]
        far_ref[1] += ones[size:]

    def body(g, carry):
        add(g * group, group)
        return carry

    lax.fori_loop(0, groups, body, 0)
    add(groups * group, NDEV - groups * group)


def grad_kernel(scale, _, own_ref, count_ref, *refs):
    pieces, rest, out_ref = refs[:NY], refs[NY:-1], refs[-1]
    own = own_ref[...]
    total = rest[0][...] if rest else jnp.zeros((ROWS, F), F32)
    for k in range(NY):
        nodes = pieces[k][...]
        score = lax.dot_general(own, nodes, NT, preferred_element_type=F32) / math.sqrt(F)
        here = slice(k * ROWS, (k + 1) * ROWS)
        grad = (count_ref[0, here, :] * jax.nn.sigmoid(score) - count_ref[1, here, :]) * scale
        high = grad.astype(BF)
        low = (grad - high.astype(F32)).astype(BF)
        total += jnp.dot(high, nodes, preferred_element_type=F32)
        total += jnp.dot(low, nodes, preferred_element_type=F32)
    out_ref[...] = total


def tiles_kernel(meta_ref, own_ref, other_ref, high_ref, low_ref, acc):
    slots = own_ref.shape[0]
    acc[...] = jnp.zeros_like(acc)
    for part, tiles_ref in enumerate((own_ref, other_ref)):

        def body(s, carry, part=part, tiles_ref=tiles_ref):
            rows = pl.ds(pl.multiple_of(meta_ref[part, s] * ROWS, ROWS), ROWS)
            dst = meta_ref[part, slots + s]
            columns = pl.ds(pl.multiple_of(part * 256 + dst * 128, 128), 128)
            acc[rows, columns] += tiles_ref[s].astype(F32)
            return carry

        lax.fori_loop(0, meta_ref[part, 2 * slots], body, 0)

    def split(k, carry):
        rows = pl.ds(pl.multiple_of(k * 128, 128), 128)
        value = acc[rows, :]
        high = value.astype(BF)
        high_ref[rows, :] = high
        low_ref[rows, :] = (value - high.astype(F32)).astype(BF)
        return carry

    lax.fori_loop(0, acc.shape[0] // 128, split, 0)


def spread_kernel(coord_ref, _, weight_ref, high_ref, low_ref, *refs):
    pre_refs, out_ref, pre = refs[:NC], refs[NC], refs[-1]
    x = coord_ref[2]
    for k in range(NC * NX):
        dc, dx = k // NX, k % NX
        place = pl.multiple_of((dc * NX + ((x + dx) & (NX - 1))) * ROWS, ROWS)
        pre[pl.ds(place, ROWS), :] = pre_refs[dc][dx * ROWS : (dx + 1) * ROWS, :]
    agg = lax.dot_general(pre[...], weight_ref[...], NT, preferred_element_type=F32).astype(BF)
    size = NZ * ROWS
    for k in range(NY):
        rows = slice(k * size, (k + 1) * size)
        part = jnp.dot(high_ref[rows, :], agg, preferred_element_type=F32)
        part += jnp.dot(low_ref[rows, :], agg, preferred_element_type=F32)
        out_ref[k] = part.astype(BF)


def terms_kernel(coord_ref, node_ref, *refs):
    pre_refs, out_refs, token_ref, terms = refs[:NC], refs[NC:-2], refs[-2], refs[-1]
    token_ref[...] = jnp.zeros_like(token_ref)
    y = coord_ref[0]
    half = NX * ROWS
    total = lax.dot_general(node_ref[:half, :], pre_refs[0][...], TN, preferred_element_type=F32)
    total += lax.dot_general(node_ref[half:, :], pre_refs[1][...], TN, preferred_element_type=F32)
    terms[...] = total
    size = ROWS // NY
    for k in range(NY):
        rows = pl.ds(pl.multiple_of(((y + k) & (NY - 1)) * size, size), size)
        out_refs[k][...] = terms[rows, :]


def plane_kernel(in_ref, out_ref):
    value = in_ref[0].astype(F32)
    for k in range(1, NY):
        value = value + in_ref[k].astype(F32)
    for k in range(NZ):
        out_ref[k] = value[k * ROWS : (k + 1) * ROWS, :].astype(BF)


def place_kernel(coord_ref, near_ref, far_ref, out_ref):
    y, c, x = coord_ref[0], coord_ref[1], coord_ref[2]
    size = ROWS // NY
    for dc, ref in enumerate((near_ref, far_ref)):
        for dx in range(NX):
            for dy in range(NY):
                start = (((x + dx) & (NX - 1)) * NC + (c ^ dc)) * ROWS + ((y + dy) & (NY - 1)) * size
                here = (dx * NY + dy) * size
                out_ref[pl.ds(pl.multiple_of(start, size), size), :] = ref[here : here + size, :]


def share_kernel(coord_ref, *refs):
    in_refs, out_ref, parts = refs[:NZ], refs[NZ], refs[-1]
    z = coord_ref[3]
    for k in range(NZ):
        parts[(z + k) & (NZ - 1)] = in_refs[k][...]
    value = parts[0]
    for k in range(1, NZ):
        value = value + parts[k]
    out_ref[...] = value


def swap(values):
    return lax.ppermute(values, "c", [(0, 1), (1, 0)])


def shift(values, axis, size, step):
    return lax.ppermute(values, axis, [(i, (i + step) % size) for i in range(size)])


def exchange(values, axes):
    return lax.all_to_all(values, axes, 0, 0, tiled=True)


def gather(values, axes, size):
    return exchange(jnp.broadcast_to(values[None], (size,) + values.shape), axes)


def pick(values, place):
    return lax.dynamic_index_in_dim(values, place, 0, keepdims=False)


def count(coord, received):
    half = jax.ShapeDtypeStruct((2, NY * ROWS, NZ * ROWS), F32)
    return pl.pallas_call(
        count_kernel,
        out_shape=[half, half, TOKEN],
        in_specs=[SMEM, VMEM],
        out_specs=[VMEM] * 3,
        scratch_shapes=[
            pltpu.VMEM((NDEV, CAP), I32),
            pltpu.VMEM((NDEV, CAP), I32),
            pltpu.VMEM((NDEV, CAP), F32),
        ],
        compiler_params=params(),
        cost_estimate=pl.CostEstimate(flops=24_000_000_000, bytes_accessed=2_400_000, transcendentals=0),
        name="count",
    )(coord, received)


def pair_grad(scale, token, own, counted, *arrays):
    return pl.pallas_call(
        functools.partial(grad_kernel, scale),
        out_shape=jax.ShapeDtypeStruct((ROWS, F), F32),
        in_specs=[ANY] + [VMEM] * (2 + len(arrays)),
        out_specs=VMEM,
        compiler_params=params(),
        cost_estimate=pl.CostEstimate(flops=3_000_000_000, bytes_accessed=3_000_000, transcendentals=131072),
        name="pair_grad",
    )(token, own, counted, *arrays)


def per_device(node_aggregate, weight, tiles, tile_src, tile_dst, tile_count, pair_owner, pair_row):
    pair_total = pair_owner.shape[0]
    slots = tiles.shape[0]
    c = lax.axis_index("c")
    coord = jnp.stack(
        [lax.axis_index("y"), c, lax.axis_index("x"), lax.axis_index("z")]
    ).astype(I32)

    with jax.named_scope("hidden"):
        pre_act = jnp.dot(node_aggregate, weight, preferred_element_type=F32)
        hidden, act_back = jax.vjp(activation, pre_act)
        hidden_b = hidden.astype(BF)

    with jax.named_scope("pair_exchange"):
        ring = gather(hidden_b, "z", NZ).reshape(NZ * ROWS, F)
        ends, token = pl.pallas_call(
            bucket_kernel,
            out_shape=[jax.ShapeDtypeStruct((NDEV, 4 * CAP), BF), TOKEN],
            in_specs=[VMEM, VMEM],
            out_specs=[VMEM, VMEM],
            scratch_shapes=[pltpu.VMEM((4 * NDEV, CAP), F32)],
            compiler_params=params(),
            cost_estimate=pl.CostEstimate(flops=9_000_000_000, bytes_accessed=400_000, transcendentals=0),
            name="bucket",
        )(pair_owner.T, pair_row.T)
        ends = ends.reshape(NDEV, 2, 2 * CAP)
        ends, late_nodes = lax.optimization_barrier((ends, node_aggregate))
        near_nodes = jnp.concatenate(
            [late_nodes] + [shift(late_nodes, "x", NX, -k) for k in range(1, NX)], axis=0
        )
        nodes = jnp.concatenate([near_nodes, swap(near_nodes)], axis=0)
        column = (lax.axis_index("x") * NC + c) * ROWS
        nodes = lax.dynamic_slice_in_dim(nodes, column, ROWS, axis=1)
        ring, ends, nodes = lax.optimization_barrier((ring, ends, nodes))
        planes = [ring] + [shift(ring, "y", NY, -k) for k in range(1, NY)]
        received = exchange(ends, ("y", "z", "c")).reshape(NDEV, 4 * CAP)
        near, far, token = count(coord, received)

    with jax.named_scope("tile_matrix"):
        halves = tiles.reshape(slots, 2, ROWS, tiles.shape[2]).transpose(1, 0, 2, 3)
        own_half = pick(halves, c)
        other_half = swap(pick(halves, 1 - c))
        meta = jnp.concatenate([tile_src, tile_dst, tile_count]).astype(I32)
        metas = jnp.stack([meta, swap(meta)])
        far_ring = swap(ring)
        *planes, token = lax.optimization_barrier((*planes, token))
        far_planes = [far_ring] + [swap(plane) for plane in planes[1:]]
    with jax.named_scope("hidden_grad"):
        scale = ROWS / (2.0 * pair_total)
        hidden_grad = pair_grad(scale, token, hidden_b, near, *planes)
        hidden_grad = pair_grad(scale, token, hidden_b, far, *far_planes, hidden_grad)
        pre_grad = act_back(hidden_grad)[0].astype(BF)
        pre_grad, metas = lax.optimization_barrier((pre_grad, metas))

    with jax.named_scope("spread"):
        high, low = pl.pallas_call(
            tiles_kernel,
            out_shape=[jax.ShapeDtypeStruct((NY * NZ * ROWS, 512), BF)] * 2,
            in_specs=[SMEM, VMEM, VMEM],
            out_specs=[VMEM] * 2,
            scratch_shapes=[pltpu.VMEM((NY * NZ * ROWS, 512), F32)],
            compiler_params=params(),
            cost_estimate=pl.CostEstimate(flops=3_000_000_000, bytes_accessed=5_000_000, transcendentals=0),
            name="tile_sum",
        )(metas, own_half, other_half)
        along_x = [pre_grad] + [shift(pre_grad, "x", NX, -k) for k in range(1, NX)]
        near_pre = jnp.concatenate(along_x, axis=0)
        pre_parts = [near_pre, swap(near_pre)]
        *terms, token = pl.pallas_call(
            terms_kernel,
            out_shape=[jax.ShapeDtypeStruct((ROWS // NY, F), F32)] * NY + [TOKEN],
            in_specs=[SMEM] + [VMEM] * 3,
            out_specs=[VMEM] * (NY + 1),
            scratch_shapes=[pltpu.VMEM((ROWS, F), F32)],
            compiler_params=params(),
            cost_estimate=pl.CostEstimate(flops=1_000_000_000, bytes_accessed=700_000, transcendentals=0),
            name="weight_terms",
        )(coord, nodes, *pre_parts)
        others = [shift(terms[k], "y", NY, k) for k in range(1, NY)]
        send = pl.pallas_call(
            spread_kernel,
            out_shape=jax.ShapeDtypeStruct((NY, NZ * ROWS, F), BF),
            in_specs=[SMEM, ANY] + [VMEM] * 5,
            out_specs=VMEM,
            scratch_shapes=[pltpu.VMEM((NC * NX * ROWS, F), BF)],
            compiler_params=params(),
            cost_estimate=pl.CostEstimate(flops=5_000_000_000, bytes_accessed=8_000_000, transcendentals=0),
            name="spread",
        )(coord, token, weight, high, low, *pre_parts)

    with jax.named_scope("sums"):
        *others, send = lax.optimization_barrier((*others, send))
        planes = exchange(send, "y")
        share = terms[0]
        for other in others:
            share = share + other
        block = pl.pallas_call(
            share_kernel,
            out_shape=jax.ShapeDtypeStruct((ROWS // NY, F), F32),
            in_specs=[SMEM] + [VMEM] * NZ,
            out_specs=VMEM,
            scratch_shapes=[pltpu.VMEM((NZ, ROWS // NY, F), F32)],
            compiler_params=params(),
            cost_estimate=pl.CostEstimate(flops=1_000_000, bytes_accessed=300_000, transcendentals=0),
            name="share_sum",
        )(coord, share, *[shift(share, "z", NZ, -k) for k in range(1, NZ)])
        part = pl.pallas_call(
            plane_kernel,
            out_shape=jax.ShapeDtypeStruct((NZ, ROWS, F), BF),
            in_specs=[VMEM],
            out_specs=VMEM,
            compiler_params=params(),
            cost_estimate=pl.CostEstimate(flops=2_000_000_000, bytes_accessed=3_000_000, transcendentals=0),
            name="plane_sum",
        )(planes)
        rings = exchange(part, "z").astype(F32)
        block = jnp.concatenate([block] + [shift(block, "y", NY, -k) for k in range(1, NY)], axis=0)
        block, part = lax.optimization_barrier((block, part))
        near_block = jnp.concatenate(
            [block] + [shift(block, "x", NX, -k) for k in range(1, NX)], axis=0
        )
        weight_grad = pl.pallas_call(
            place_kernel,
            out_shape=jax.ShapeDtypeStruct((F, F), F32),
            in_specs=[SMEM, VMEM, VMEM],
            out_specs=VMEM,
            compiler_params=params(),
            cost_estimate=pl.CostEstimate(flops=1_000_000, bytes_accessed=2_000_000, transcendentals=0),
            name="place",
        )(coord, near_block, swap(near_block))
        feature_grad = jnp.sum(rings, axis=0).astype(BF)
    return (feature_grad, weight_grad)


def solution(mesh):
    grid = Mesh(mesh.devices.reshape(NX, NY, NZ, NC), ("x", "y", "z", "c"))
    split = P(("x", "y", "z", "c"))
    return jax.shard_map(
        per_device,
        mesh=grid,
        in_specs=(split, P(), split, split, split, split, split, split),
        out_specs=(split, P()),
        check_vma=False,
    )
```

```python
import functools
import math

import jax
import jax.numpy as jnp
from jax import lax
from jax.experimental import pallas as pl
from jax.experimental.pallas import tpu as pltpu
from jax.sharding import Mesh, PartitionSpec as P

NX, NY, NZ, NC = 4, 4, 8, 2
NDEV = NY * NZ * NC
ROWS = 64
F = 512
CAP = 512
BF = jnp.bfloat16
F32 = jnp.float32
I32 = jnp.int32
POS = 4096.0
SUB = 256
SUBS = 8
NT = (((1,), (1,)), ((), ()))
TN = (((0,), (0,)), ((), ()))
VMEM = pl.BlockSpec(memory_space=pltpu.VMEM)
SMEM = pl.BlockSpec(memory_space=pltpu.SMEM)
ANY = pl.BlockSpec(memory_space=pl.ANY)


TOKEN = jax.ShapeDtypeStruct((8, 128), F32)


def params(mib=16):
    return pltpu.CompilerParams(vmem_limit_bytes=mib << 20)


def activation(values):
    return jax.nn.gelu(values)


def bucket_kernel(owner_ref, row_ref, out_ref, token_ref, acc):
    token_ref[...] = jnp.zeros_like(token_ref)
    total = owner_ref.shape[1]
    positives = total // 5
    step = SUB * SUBS
    tri = (
        lax.broadcasted_iota(I32, (SUB, SUB), 0) < lax.broadcasted_iota(I32, (SUB, SUB), 1)
    ).astype(BF)
    acc[...] = jnp.zeros_like(acc)
    base = jnp.zeros((NDEV, 1), F32)
    for end in range(2):

        def body(j, base, end=end):
            ranks, parts = [], [[], [], [], []]
            for s in range(SUBS):
                start = pl.multiple_of(j * step + s * SUB, SUB)
                here = pl.ds(start, SUB)
                own = owner_ref[end : end + 1, here]
                same = lax.broadcasted_iota(I32, (NDEV, SUB), 0) == own
                hot = same.astype(F32)
                prefix = jnp.dot(hot.astype(BF), tri, preferred_element_type=F32)
                ranks.append(jnp.sum(hot * (prefix + base), axis=0, keepdims=True))
                base = base + jnp.sum(hot, axis=1, keepdims=True)
                place = start + lax.broadcasted_iota(I32, (1, SUB), 1)
                weight = jnp.where(place < positives, POS, 1.0)
                values = [
                    weight,
                    row_ref[end : end + 1, here].astype(F32),
                    owner_ref[1 - end : 2 - end, here].astype(F32),
                    row_ref[1 - end : 2 - end, here].astype(F32),
                ]
                for v in range(4):
                    parts[v].append((hot * values[v]).astype(BF))
            left = jnp.concatenate([jnp.concatenate(p, axis=1) for p in parts], axis=0)
            rank = jnp.concatenate(ranks, axis=1).astype(I32)
            right = (lax.broadcasted_iota(I32, (CAP, step), 0) == rank).astype(F32).astype(BF)
            acc[...] += lax.dot_general(left, right, NT, preferred_element_type=F32)
            return base

        base = lax.fori_loop(0, total // step, body, base)
    for v in range(4):
        out_ref[:, v * CAP : (v + 1) * CAP] = acc[v * NDEV : (v + 1) * NDEV, :].astype(BF)


def count_kernel(coord_ref, recv_ref, near_ref, far_ref, token_ref, left_at, right_at, weight_at):
    token_ref[...] = jnp.zeros_like(token_ref)
    y, c = coord_ref[0], coord_ref[1]
    weight_at[...] = recv_ref[:, 0:CAP].astype(F32)
    own_row = recv_ref[:, CAP : 2 * CAP].astype(F32).astype(I32)
    owner = recv_ref[:, 2 * CAP : 3 * CAP].astype(F32).astype(I32)
    row = recv_ref[:, 3 * CAP : 4 * CAP].astype(F32).astype(I32)
    piece = ((owner & 1) ^ c) * NY + (((owner >> 4) - y) & (NY - 1))
    left_at[...] = piece * ROWS + own_row
    right_at[...] = ((owner >> 1) & (NZ - 1)) * ROWS + row
    near_ref[...] = jnp.zeros_like(near_ref)
    far_ref[...] = jnp.zeros_like(far_ref)
    group = 7
    groups = NDEV // group
    size = NY * ROWS

    def add(start, count):
        spots = lax.broadcasted_iota(I32, (CAP, CAP), 0)
        left, right = [], []
        for s in range(count):
            here = pl.ds(start + s, 1)
            left.append(jnp.where(spots == left_at[here, :], weight_at[here, :], 0.0).astype(BF))
            right.append(jnp.where(spots == right_at[here, :], 1.0, 0.0).astype(BF))
        total = lax.dot_general(
            jnp.concatenate(left, axis=1), jnp.concatenate(right, axis=1), NT, preferred_element_type=F32
        )
        ones = jnp.floor(total * (1.0 / POS))
        both = total - (POS - 1.0) * ones
        near_ref[0] += both[:size]
        near_ref[1] += ones[:size]
        far_ref[0] += both[size:]
        far_ref[1] += ones[size:]

    def body(g, carry):
        add(g * group, group)
        return carry

    lax.fori_loop(0, groups, body, 0)
    add(groups * group, NDEV - groups * group)


def grad_kernel(scale, _, own_ref, count_ref, *refs):
    pieces, rest, out_ref = refs[:NY], refs[NY:-1], refs[-1]
    own = own_ref[...]
    total = rest[0][...] if rest else jnp.zeros((ROWS, F), F32)
    for k in range(NY):
        nodes = pieces[k][...]
        score = lax.dot_general(own, nodes, NT, preferred_element_type=F32) / math.sqrt(F)
        here = slice(k * ROWS, (k + 1) * ROWS)
        grad = (count_ref[0, here, :] * jax.nn.sigmoid(score) - count_ref[1, here, :]) * scale
        high = grad.astype(BF)
        low = (grad - high.astype(F32)).astype(BF)
        total += jnp.dot(high, nodes, preferred_element_type=F32)
        total += jnp.dot(low, nodes, preferred_element_type=F32)
    out_ref[...] = total


def tiles_kernel(meta_ref, own_ref, other_ref, high_ref, low_ref, token_ref, acc):
    token_ref[...] = jnp.zeros_like(token_ref)
    slots = own_ref.shape[0]
    acc[...] = jnp.zeros_like(acc)
    for part, tiles_ref in enumerate((own_ref, other_ref)):

        def body(s, carry, part=part, tiles_ref=tiles_ref):
            rows = pl.ds(pl.multiple_of(meta_ref[part, s] * ROWS, ROWS), ROWS)
            dst = meta_ref[part, slots + s]
            columns = pl.ds(pl.multiple_of(part * 256 + dst * 128, 128), 128)
            acc[rows, columns] += tiles_ref[s].astype(F32)
            return carry

        lax.fori_loop(0, meta_ref[part, 2 * slots], body, 0)

    def split(k, carry):
        rows = pl.ds(pl.multiple_of(k * 128, 128), 128)
        value = acc[rows, :]
        high = value.astype(BF)
        high_ref[rows, :] = high
        low_ref[rows, :] = (value - high.astype(F32)).astype(BF)
        return carry

    lax.fori_loop(0, acc.shape[0] // 128, split, 0)


def spread_kernel(coord_ref, _, weight_ref, high_ref, low_ref, *refs):
    pre_refs, out_ref, pre = refs[: NC * NX], refs[-2], refs[-1]
    x = coord_ref[2]
    for k in range(NC * NX):
        dc, dx = k // NX, k % NX
        place = pl.multiple_of((dc * NX + ((x + dx) & (NX - 1))) * ROWS, ROWS)
        pre[pl.ds(place, ROWS), :] = pre_refs[k][...]
    agg = lax.dot_general(pre[...], weight_ref[...], NT, preferred_element_type=F32).astype(BF)
    size = NZ * ROWS
    for k in range(NY):
        rows = slice(k * size, (k + 1) * size)
        part = jnp.dot(high_ref[rows, :], agg, preferred_element_type=F32)
        part += jnp.dot(low_ref[rows, :], agg, preferred_element_type=F32)
        out_ref[k] = part.astype(BF)


def terms_kernel(coord_ref, _, *refs):
    pieces = NC * NX
    node_refs, pre_refs = refs[:pieces], refs[pieces : 2 * pieces]
    out_refs, token_ref, terms = refs[2 * pieces : -2], refs[-2], refs[-1]
    token_ref[...] = jnp.zeros_like(token_ref)
    y, c, x = coord_ref[0], coord_ref[1], coord_ref[2]
    columns = pl.ds(pl.multiple_of(x * NC * ROWS, NC * ROWS), NC * ROWS)
    node = jnp.concatenate([ref[:, columns] for ref in node_refs], axis=0)
    pre = jnp.concatenate([ref[...] for ref in pre_refs], axis=0)
    terms[...] = lax.dot_general(node, pre, TN, preferred_element_type=F32)
    size = ROWS // NY
    for k in range(NY):
        start = c * ROWS + ((y + k) & (NY - 1)) * size
        out_refs[k][...] = terms[pl.ds(pl.multiple_of(start, size), size), :]


def plane_kernel(in_ref, out_ref):
    value = in_ref[0].astype(F32)
    for k in range(1, NY):
        value = value + in_ref[k].astype(F32)
    for k in range(NZ):
        out_ref[k] = value[k * ROWS : (k + 1) * ROWS, :].astype(BF)


def place_kernel(coord_ref, near_ref, far_ref, out_ref):
    y, c, x = coord_ref[0], coord_ref[1], coord_ref[2]
    size = ROWS // NY
    for dc, ref in enumerate((near_ref, far_ref)):
        for dx in range(NX):
            for dy in range(NY):
                start = (((x + dx) & (NX - 1)) * NC + (c ^ dc)) * ROWS + ((y + dy) & (NY - 1)) * size
                here = (dx * NY + dy) * size
                out_ref[pl.ds(pl.multiple_of(start, size), size), :] = ref[here : here + size, :]


def share_kernel(coord_ref, *refs):
    in_refs, out_ref, parts = refs[:NZ], refs[NZ], refs[-1]
    z = coord_ref[3]
    for k in range(NZ):
        parts[(z + k) & (NZ - 1)] = in_refs[k][...]
    value = parts[0]
    for k in range(1, NZ):
        value = value + parts[k]
    out_ref[...] = value


def swap(values):
    return lax.ppermute(values, "c", [(0, 1), (1, 0)])


def shift(values, axis, size, step):
    return lax.ppermute(values, axis, [(i, (i + step) % size) for i in range(size)])


def exchange(values, axes):
    return lax.all_to_all(values, axes, 0, 0, tiled=True)


def gather(values, axes, size):
    return exchange(jnp.broadcast_to(values[None], (size,) + values.shape), axes)


def pick(values, place):
    return lax.dynamic_index_in_dim(values, place, 0, keepdims=False)


def count(coord, received):
    half = jax.ShapeDtypeStruct((2, NY * ROWS, NZ * ROWS), F32)
    return pl.pallas_call(
        count_kernel,
        out_shape=[half, half, TOKEN],
        in_specs=[SMEM, VMEM],
        out_specs=[VMEM] * 3,
        scratch_shapes=[
            pltpu.VMEM((NDEV, CAP), I32),
            pltpu.VMEM((NDEV, CAP), I32),
            pltpu.VMEM((NDEV, CAP), F32),
        ],
        compiler_params=params(),
        cost_estimate=pl.CostEstimate(flops=24_000_000_000, bytes_accessed=2_400_000, transcendentals=0),
        name="count",
    )(coord, received)


def pair_grad(scale, token, own, counted, *arrays):
    return pl.pallas_call(
        functools.partial(grad_kernel, scale),
        out_shape=jax.ShapeDtypeStruct((ROWS, F), F32),
        in_specs=[ANY] + [VMEM] * (2 + len(arrays)),
        out_specs=VMEM,
        compiler_params=params(),
        cost_estimate=pl.CostEstimate(flops=3_000_000_000, bytes_accessed=3_000_000, transcendentals=131072),
        name="pair_grad",
    )(token, own, counted, *arrays)


def per_device(node_aggregate, weight, tiles, tile_src, tile_dst, tile_count, pair_owner, pair_row):
    pair_total = pair_owner.shape[0]
    slots = tiles.shape[0]
    c = lax.axis_index("c")
    coord = jnp.stack(
        [lax.axis_index("y"), c, lax.axis_index("x"), lax.axis_index("z")]
    ).astype(I32)

    with jax.named_scope("hidden"):
        pre_act = jnp.dot(node_aggregate, weight, preferred_element_type=F32)
        hidden, act_back = jax.vjp(activation, pre_act)
        hidden_b = hidden.astype(BF)

    with jax.named_scope("pair_exchange"):
        ends, token = pl.pallas_call(
            bucket_kernel,
            out_shape=[jax.ShapeDtypeStruct((NDEV, 4 * CAP), BF), TOKEN],
            in_specs=[VMEM, VMEM],
            out_specs=[VMEM, VMEM],
            scratch_shapes=[pltpu.VMEM((4 * NDEV, CAP), F32)],
            compiler_params=params(),
            cost_estimate=pl.CostEstimate(flops=9_000_000_000, bytes_accessed=400_000, transcendentals=0),
            name="bucket",
        )(pair_owner.T, pair_row.T)
        ends = ends.reshape(NDEV, 2, 2 * CAP)
        hidden_b, late_nodes = lax.optimization_barrier((hidden_b, node_aggregate))
        ring = gather(hidden_b, "z", NZ).reshape(NZ * ROWS, F)
        nodes = [late_nodes] + [shift(late_nodes, "x", NX, -k) for k in range(1, NX)]
        nodes = nodes + [swap(node) for node in nodes]
        ring, ends, *nodes = lax.optimization_barrier((ring, ends, *nodes))
        planes = [ring] + [shift(ring, "y", NY, -k) for k in range(1, NY)]
        received = exchange(ends, ("y", "z", "c")).reshape(NDEV, 4 * CAP)
        near, far, token = count(coord, received)

    with jax.named_scope("tile_matrix"):
        halves = tiles.reshape(slots, 2, ROWS, tiles.shape[2]).transpose(1, 0, 2, 3)
        own_half = pick(halves, c)
        other_half = swap(pick(halves, 1 - c))
        meta = jnp.concatenate([tile_src, tile_dst, tile_count]).astype(I32)
        metas = jnp.stack([meta, swap(meta)])
        far_ring = swap(ring)
        *planes, token = lax.optimization_barrier((*planes, token))
        far_planes = [far_ring] + [swap(plane) for plane in planes[1:]]
    with jax.named_scope("hidden_grad"):
        scale = ROWS / (2.0 * pair_total)
        hidden_grad = pair_grad(scale, token, hidden_b, near, *planes)
        hidden_grad = pair_grad(scale, token, hidden_b, far, *far_planes, hidden_grad)
        pre_grad = act_back(hidden_grad)[0].astype(BF)
        pre_grad, metas = lax.optimization_barrier((pre_grad, metas))

    with jax.named_scope("spread"):
        high, low, tile_token = pl.pallas_call(
            tiles_kernel,
            out_shape=[jax.ShapeDtypeStruct((NY * NZ * ROWS, 512), BF)] * 2 + [TOKEN],
            in_specs=[SMEM, VMEM, VMEM],
            out_specs=[VMEM] * 3,
            scratch_shapes=[pltpu.VMEM((NY * NZ * ROWS, 512), F32)],
            compiler_params=params(),
            cost_estimate=pl.CostEstimate(flops=3_000_000_000, bytes_accessed=5_000_000, transcendentals=0),
            name="tile_sum",
        )(metas, own_half, other_half)
        along_x = [shift(pre_grad, "x", NX, -k) for k in range(1, NX)]
        *along_x, tile_token = lax.optimization_barrier((*along_x, tile_token))
        pre_parts = [pre_grad] + along_x
        pre_parts = pre_parts + [swap(part) for part in pre_parts]
        *terms, token = pl.pallas_call(
            terms_kernel,
            out_shape=[jax.ShapeDtypeStruct((ROWS // NY, F), F32)] * NY + [TOKEN],
            in_specs=[SMEM, ANY] + [VMEM] * (2 * NC * NX),
            out_specs=[VMEM] * (NY + 1),
            scratch_shapes=[pltpu.VMEM((NC * ROWS, F), F32)],
            compiler_params=params(),
            cost_estimate=pl.CostEstimate(flops=1_000_000_000, bytes_accessed=700_000, transcendentals=0),
            name="weight_terms",
        )(coord, tile_token, *nodes, *pre_parts)
        others = [shift(terms[k], "y", NY, k) for k in range(1, NY)]
        send = pl.pallas_call(
            spread_kernel,
            out_shape=jax.ShapeDtypeStruct((NY, NZ * ROWS, F), BF),
            in_specs=[SMEM, ANY] + [VMEM] * (3 + NC * NX),
            out_specs=VMEM,
            scratch_shapes=[pltpu.VMEM((NC * NX * ROWS, F), BF)],
            compiler_params=params(),
            cost_estimate=pl.CostEstimate(flops=5_000_000_000, bytes_accessed=8_000_000, transcendentals=0),
            name="spread",
        )(coord, token, weight, high, low, *pre_parts)

    with jax.named_scope("sums"):
        *others, send = lax.optimization_barrier((*others, send))
        planes = exchange(send, "y")
        share = terms[0]
        for other in others:
            share = share + other
        block = pl.pallas_call(
            share_kernel,
            out_shape=jax.ShapeDtypeStruct((ROWS // NY, F), F32),
            in_specs=[SMEM] + [VMEM] * NZ,
            out_specs=VMEM,
            scratch_shapes=[pltpu.VMEM((NZ, ROWS // NY, F), F32)],
            compiler_params=params(),
            cost_estimate=pl.CostEstimate(flops=1_000_000, bytes_accessed=300_000, transcendentals=0),
            name="share_sum",
        )(coord, share, *[shift(share, "z", NZ, -k) for k in range(1, NZ)])
        part = pl.pallas_call(
            plane_kernel,
            out_shape=jax.ShapeDtypeStruct((NZ, ROWS, F), BF),
            in_specs=[VMEM],
            out_specs=VMEM,
            compiler_params=params(),
            cost_estimate=pl.CostEstimate(flops=2_000_000_000, bytes_accessed=3_000_000, transcendentals=0),
            name="plane_sum",
        )(planes)
        rings = exchange(part, "z").astype(F32)
        block = jnp.concatenate([block] + [shift(block, "y", NY, -k) for k in range(1, NY)], axis=0)
        block, part = lax.optimization_barrier((block, part))
        near_block = jnp.concatenate(
            [block] + [shift(block, "x", NX, -k) for k in range(1, NX)], axis=0
        )
        weight_grad = pl.pallas_call(
            place_kernel,
            out_shape=jax.ShapeDtypeStruct((F, F), F32),
            in_specs=[SMEM, VMEM, VMEM],
            out_specs=VMEM,
            compiler_params=params(),
            cost_estimate=pl.CostEstimate(flops=1_000_000, bytes_accessed=2_000_000, transcendentals=0),
            name="place",
        )(coord, near_block, swap(near_block))
        feature_grad = jnp.sum(rings, axis=0).astype(BF)
    return (feature_grad, weight_grad)


def solution(mesh):
    grid = Mesh(mesh.devices.reshape(NX, NY, NZ, NC), ("x", "y", "z", "c"))
    split = P(("x", "y", "z", "c"))
    return jax.shard_map(
        per_device,
        mesh=grid,
        in_specs=(split, P(), split, split, split, split, split, split),
        out_specs=(split, P()),
        check_vma=False,
    )
```

```python
import functools
import math

import jax
import jax.numpy as jnp
from jax import lax
from jax.experimental import pallas as pl
from jax.experimental.pallas import tpu as pltpu
from jax.sharding import Mesh, PartitionSpec as P

NX, NY, NZ, NC = 4, 4, 8, 2
NDEV = NY * NZ * NC
ROWS = 64
F = 512
CAP = 512
BF = jnp.bfloat16
F32 = jnp.float32
I32 = jnp.int32
POS = 4096.0
SUB = 256
SUBS = 8
NT = (((1,), (1,)), ((), ()))
TN = (((0,), (0,)), ((), ()))
VMEM = pl.BlockSpec(memory_space=pltpu.VMEM)
SMEM = pl.BlockSpec(memory_space=pltpu.SMEM)
ANY = pl.BlockSpec(memory_space=pl.ANY)


TOKEN = jax.ShapeDtypeStruct((8, 128), F32)


def params(mib=16):
    return pltpu.CompilerParams(vmem_limit_bytes=mib << 20)


def activation(values):
    return jax.nn.gelu(values)


def bucket_kernel(owner_ref, row_ref, out_ref, token_ref, acc):
    token_ref[...] = jnp.zeros_like(token_ref)
    total = owner_ref.shape[1]
    positives = total // 5
    step = SUB * SUBS
    tri = (
        lax.broadcasted_iota(I32, (SUB, SUB), 0) < lax.broadcasted_iota(I32, (SUB, SUB), 1)
    ).astype(BF)
    acc[...] = jnp.zeros_like(acc)
    base = jnp.zeros((NDEV, 1), F32)
    for end in range(2):

        def body(j, base, end=end):
            ranks, parts = [], [[], [], [], []]
            for s in range(SUBS):
                start = pl.multiple_of(j * step + s * SUB, SUB)
                here = pl.ds(start, SUB)
                own = owner_ref[end : end + 1, here]
                same = lax.broadcasted_iota(I32, (NDEV, SUB), 0) == own
                hot = same.astype(F32)
                prefix = jnp.dot(hot.astype(BF), tri, preferred_element_type=F32)
                ranks.append(jnp.sum(hot * (prefix + base), axis=0, keepdims=True))
                base = base + jnp.sum(hot, axis=1, keepdims=True)
                place = start + lax.broadcasted_iota(I32, (1, SUB), 1)
                weight = jnp.where(place < positives, POS, 1.0)
                values = [
                    weight,
                    row_ref[end : end + 1, here].astype(F32),
                    owner_ref[1 - end : 2 - end, here].astype(F32),
                    row_ref[1 - end : 2 - end, here].astype(F32),
                ]
                for v in range(4):
                    parts[v].append((hot * values[v]).astype(BF))
            left = jnp.concatenate([jnp.concatenate(p, axis=1) for p in parts], axis=0)
            rank = jnp.concatenate(ranks, axis=1).astype(I32)
            right = (lax.broadcasted_iota(I32, (CAP, step), 0) == rank).astype(F32).astype(BF)
            acc[...] += lax.dot_general(left, right, NT, preferred_element_type=F32)
            return base

        base = lax.fori_loop(0, total // step, body, base)
    for v in range(4):
        out_ref[:, v * CAP : (v + 1) * CAP] = acc[v * NDEV : (v + 1) * NDEV, :].astype(BF)


def count_kernel(coord_ref, recv_ref, near_ref, far_ref, token_ref, left_at, right_at, weight_at):
    token_ref[...] = jnp.zeros_like(token_ref)
    y, c = coord_ref[0], coord_ref[1]
    weight_at[...] = recv_ref[:, 0:CAP].astype(F32)
    own_row = recv_ref[:, CAP : 2 * CAP].astype(F32).astype(I32)
    owner = recv_ref[:, 2 * CAP : 3 * CAP].astype(F32).astype(I32)
    row = recv_ref[:, 3 * CAP : 4 * CAP].astype(F32).astype(I32)
    piece = ((owner & 1) ^ c) * NY + (((owner >> 4) - y) & (NY - 1))
    left_at[...] = piece * ROWS + own_row
    right_at[...] = ((owner >> 1) & (NZ - 1)) * ROWS + row
    near_ref[...] = jnp.zeros_like(near_ref)
    far_ref[...] = jnp.zeros_like(far_ref)
    group = 7
    groups = NDEV // group
    size = NY * ROWS

    def add(start, count):
        spots = lax.broadcasted_iota(I32, (CAP, CAP), 0)
        left, right = [], []
        for s in range(count):
            here = pl.ds(start + s, 1)
            left.append(jnp.where(spots == left_at[here, :], weight_at[here, :], 0.0).astype(BF))
            right.append(jnp.where(spots == right_at[here, :], 1.0, 0.0).astype(BF))
        total = lax.dot_general(
            jnp.concatenate(left, axis=1), jnp.concatenate(right, axis=1), NT, preferred_element_type=F32
        )
        ones = jnp.floor(total * (1.0 / POS))
        both = total - (POS - 1.0) * ones
        near_ref[0] += both[:size]
        near_ref[1] += ones[:size]
        far_ref[0] += both[size:]
        far_ref[1] += ones[size:]

    def body(g, carry):
        add(g * group, group)
        return carry

    lax.fori_loop(0, groups, body, 0)
    add(groups * group, NDEV - groups * group)


def grad_kernel(scale, _, own_ref, count_ref, *refs):
    pieces, rest, out_ref = refs[:NY], refs[NY:-1], refs[-1]
    own = own_ref[...]
    total = rest[0][...] if rest else jnp.zeros((ROWS, F), F32)
    for k in range(NY):
        nodes = pieces[k][...]
        score = lax.dot_general(own, nodes, NT, preferred_element_type=F32) / math.sqrt(F)
        here = slice(k * ROWS, (k + 1) * ROWS)
        grad = (count_ref[0, here, :] * jax.nn.sigmoid(score) - count_ref[1, here, :]) * scale
        high = grad.astype(BF)
        low = (grad - high.astype(F32)).astype(BF)
        total += jnp.dot(high, nodes, preferred_element_type=F32)
        total += jnp.dot(low, nodes, preferred_element_type=F32)
    out_ref[...] = total


def tiles_kernel(meta_ref, own_ref, other_ref, high_ref, low_ref, token_ref, acc):
    token_ref[...] = jnp.zeros_like(token_ref)
    slots = own_ref.shape[0]
    acc[...] = jnp.zeros_like(acc)
    for part, tiles_ref in enumerate((own_ref, other_ref)):

        def body(s, carry, part=part, tiles_ref=tiles_ref):
            rows = pl.ds(pl.multiple_of(meta_ref[part, s] * ROWS, ROWS), ROWS)
            dst = meta_ref[part, slots + s]
            columns = pl.ds(pl.multiple_of(part * 256 + dst * 128, 128), 128)
            acc[rows, columns] += tiles_ref[s].astype(F32)
            return carry

        lax.fori_loop(0, meta_ref[part, 2 * slots], body, 0)

    def split(k, carry):
        rows = pl.ds(pl.multiple_of(k * 128, 128), 128)
        value = acc[rows, :]
        high = value.astype(BF)
        high_ref[rows, :] = high
        low_ref[rows, :] = (value - high.astype(F32)).astype(BF)
        return carry

    lax.fori_loop(0, acc.shape[0] // 128, split, 0)


def spread_kernel(coord_ref, _, weight_ref, high_ref, low_ref, *refs):
    pre_refs, out_ref, pre = refs[: NC * NX], refs[-2], refs[-1]
    x = coord_ref[2]
    for k in range(NC * NX):
        dc, dx = k // NX, k % NX
        place = pl.multiple_of((dc * NX + ((x + dx) & (NX - 1))) * ROWS, ROWS)
        pre[pl.ds(place, ROWS), :] = pre_refs[k][:, :F]
    agg = lax.dot_general(pre[...], weight_ref[...], NT, preferred_element_type=F32).astype(BF)
    size = NZ * ROWS
    for k in range(NY):
        rows = slice(k * size, (k + 1) * size)
        part = jnp.dot(high_ref[rows, :], agg, preferred_element_type=F32)
        part += jnp.dot(low_ref[rows, :], agg, preferred_element_type=F32)
        out_ref[k] = part.astype(BF)


def terms_kernel(coord_ref, _, *refs):
    part_refs, out_refs = refs[: NC * NX], refs[NC * NX : -2]
    token_ref, terms = refs[-2:]
    token_ref[...] = jnp.zeros_like(token_ref)
    y, c = coord_ref[0], coord_ref[1]
    node = jnp.concatenate([ref[:, F:] for ref in part_refs], axis=0)
    pre = jnp.concatenate([ref[:, :F] for ref in part_refs], axis=0)
    terms[...] = lax.dot_general(node, pre, TN, preferred_element_type=F32)
    size = ROWS // NY
    for k in range(NY):
        start = c * ROWS + ((y + k) & (NY - 1)) * size
        out_refs[k][...] = terms[pl.ds(pl.multiple_of(start, size), size), :]


def plane_kernel(in_ref, out_ref):
    value = in_ref[0].astype(F32)
    for k in range(1, NY):
        value = value + in_ref[k].astype(F32)
    for k in range(NZ):
        out_ref[k] = value[k * ROWS : (k + 1) * ROWS, :].astype(BF)


def place_kernel(coord_ref, near_ref, far_ref, out_ref):
    y, c, x = coord_ref[0], coord_ref[1], coord_ref[2]
    size = ROWS // NY
    for dc, ref in enumerate((near_ref, far_ref)):
        for dx in range(NX):
            for dy in range(NY):
                start = (((x + dx) & (NX - 1)) * NC + (c ^ dc)) * ROWS + ((y + dy) & (NY - 1)) * size
                here = (dx * NY + dy) * size
                out_ref[pl.ds(pl.multiple_of(start, size), size), :] = ref[here : here + size, :]


def share_kernel(coord_ref, *refs):
    in_refs, out_ref, parts = refs[:NZ], refs[NZ], refs[-1]
    z = coord_ref[3]
    for k in range(NZ):
        parts[(z + k) & (NZ - 1)] = in_refs[k][...]
    value = parts[0]
    for k in range(1, NZ):
        value = value + parts[k]
    out_ref[...] = value


def swap(values):
    return lax.ppermute(values, "c", [(0, 1), (1, 0)])


def shift(values, axis, size, step):
    return lax.ppermute(values, axis, [(i, (i + step) % size) for i in range(size)])


def exchange(values, axes):
    return lax.all_to_all(values, axes, 0, 0, tiled=True)


def gather(values, axes, size):
    return exchange(jnp.broadcast_to(values[None], (size,) + values.shape), axes)


def pick(values, place):
    return lax.dynamic_index_in_dim(values, place, 0, keepdims=False)


def count(coord, received):
    half = jax.ShapeDtypeStruct((2, NY * ROWS, NZ * ROWS), F32)
    return pl.pallas_call(
        count_kernel,
        out_shape=[half, half, TOKEN],
        in_specs=[SMEM, VMEM],
        out_specs=[VMEM] * 3,
        scratch_shapes=[
            pltpu.VMEM((NDEV, CAP), I32),
            pltpu.VMEM((NDEV, CAP), I32),
            pltpu.VMEM((NDEV, CAP), F32),
        ],
        compiler_params=params(),
        cost_estimate=pl.CostEstimate(flops=24_000_000_000, bytes_accessed=2_400_000, transcendentals=0),
        name="count",
    )(coord, received)


def pair_grad(scale, token, own, counted, *arrays):
    return pl.pallas_call(
        functools.partial(grad_kernel, scale),
        out_shape=jax.ShapeDtypeStruct((ROWS, F), F32),
        in_specs=[ANY] + [VMEM] * (2 + len(arrays)),
        out_specs=VMEM,
        compiler_params=params(),
        cost_estimate=pl.CostEstimate(flops=3_000_000_000, bytes_accessed=3_000_000, transcendentals=131072),
        name="pair_grad",
    )(token, own, counted, *arrays)


def per_device(node_aggregate, weight, tiles, tile_src, tile_dst, tile_count, pair_owner, pair_row):
    pair_total = pair_owner.shape[0]
    slots = tiles.shape[0]
    c = lax.axis_index("c")
    coord = jnp.stack(
        [lax.axis_index("y"), c, lax.axis_index("x"), lax.axis_index("z")]
    ).astype(I32)

    with jax.named_scope("hidden"):
        pre_act = jnp.dot(node_aggregate, weight, preferred_element_type=F32)
        hidden, act_back = jax.vjp(activation, pre_act)
        hidden_b = hidden.astype(BF)

    with jax.named_scope("pair_exchange"):
        ends, token = pl.pallas_call(
            bucket_kernel,
            out_shape=[jax.ShapeDtypeStruct((NDEV, 4 * CAP), BF), TOKEN],
            in_specs=[VMEM, VMEM],
            out_specs=[VMEM, VMEM],
            scratch_shapes=[pltpu.VMEM((4 * NDEV, CAP), F32)],
            compiler_params=params(),
            cost_estimate=pl.CostEstimate(flops=9_000_000_000, bytes_accessed=400_000, transcendentals=0),
            name="bucket",
        )(pair_owner.T, pair_row.T)
        ends = ends.reshape(NDEV, 2, 2 * CAP)
        ring = gather(hidden_b, "z", NZ).reshape(NZ * ROWS, F)
        ring, ends = lax.optimization_barrier((ring, ends))
        planes = [ring] + [shift(ring, "y", NY, -k) for k in range(1, NY)]
        received = exchange(ends, ("y", "z", "c")).reshape(NDEV, 4 * CAP)
        near, far, token = count(coord, received)

    with jax.named_scope("tile_matrix"):
        halves = tiles.reshape(slots, 2, ROWS, tiles.shape[2]).transpose(1, 0, 2, 3)
        own_half = pick(halves, c)
        other_half = swap(pick(halves, 1 - c))
        meta = jnp.concatenate([tile_src, tile_dst, tile_count]).astype(I32)
        metas = jnp.stack([meta, swap(meta)])
        far_ring = swap(ring)
        *planes, token = lax.optimization_barrier((*planes, token))
        far_planes = [far_ring] + [swap(plane) for plane in planes[1:]]
    with jax.named_scope("hidden_grad"):
        scale = ROWS / (2.0 * pair_total)
        hidden_grad = pair_grad(scale, token, hidden_b, near, *planes)
        hidden_grad = pair_grad(scale, token, hidden_b, far, *far_planes, hidden_grad)
        pre_grad = act_back(hidden_grad)[0].astype(BF)
        pre_grad, metas = lax.optimization_barrier((pre_grad, metas))

    with jax.named_scope("spread"):
        high, low, tile_token = pl.pallas_call(
            tiles_kernel,
            out_shape=[jax.ShapeDtypeStruct((NY * NZ * ROWS, 512), BF)] * 2 + [TOKEN],
            in_specs=[SMEM, VMEM, VMEM],
            out_specs=[VMEM] * 3,
            scratch_shapes=[pltpu.VMEM((NY * NZ * ROWS, 512), F32)],
            compiler_params=params(),
            cost_estimate=pl.CostEstimate(flops=3_000_000_000, bytes_accessed=5_000_000, transcendentals=0),
            name="tile_sum",
        )(metas, own_half, other_half)
        width = F // NX
        x = lax.axis_index("x")
        rows = []
        for k in range(NX):
            there = ((x - k) & (NX - 1)) * width
            node = lax.dynamic_slice_in_dim(node_aggregate, there, width, axis=1)
            rows.append(jnp.concatenate([pre_grad, node], axis=1))
        along_x = [shift(rows[k], "x", NX, -k) for k in range(1, NX)]
        *along_x, tile_token = lax.optimization_barrier((*along_x, tile_token))
        parts = [rows[0]] + along_x
        parts = parts + [swap(part) for part in parts]
        *terms, token = pl.pallas_call(
            terms_kernel,
            out_shape=[jax.ShapeDtypeStruct((ROWS // NY, F), F32)] * NY + [TOKEN],
            in_specs=[SMEM, ANY] + [VMEM] * (NC * NX),
            out_specs=[VMEM] * (NY + 1),
            scratch_shapes=[pltpu.VMEM((NC * ROWS, F), F32)],
            compiler_params=params(),
            cost_estimate=pl.CostEstimate(flops=1_000_000_000, bytes_accessed=700_000, transcendentals=0),
            name="weight_terms",
        )(coord, tile_token, *parts)
        others = [shift(terms[k], "y", NY, k) for k in range(1, NY)]
        send = pl.pallas_call(
            spread_kernel,
            out_shape=jax.ShapeDtypeStruct((NY, NZ * ROWS, F), BF),
            in_specs=[SMEM, ANY] + [VMEM] * (3 + NC * NX),
            out_specs=VMEM,
            scratch_shapes=[pltpu.VMEM((NC * NX * ROWS, F), BF)],
            compiler_params=params(),
            cost_estimate=pl.CostEstimate(flops=5_000_000_000, bytes_accessed=8_000_000, transcendentals=0),
            name="spread",
        )(coord, token, weight, high, low, *parts)

    with jax.named_scope("sums"):
        *others, send = lax.optimization_barrier((*others, send))
        planes = exchange(send, "y")
        share = terms[0]
        for other in others:
            share = share + other
        block = pl.pallas_call(
            share_kernel,
            out_shape=jax.ShapeDtypeStruct((ROWS // NY, F), F32),
            in_specs=[SMEM] + [VMEM] * NZ,
            out_specs=VMEM,
            scratch_shapes=[pltpu.VMEM((NZ, ROWS // NY, F), F32)],
            compiler_params=params(),
            cost_estimate=pl.CostEstimate(flops=1_000_000, bytes_accessed=300_000, transcendentals=0),
            name="share_sum",
        )(coord, share, *[shift(share, "z", NZ, -k) for k in range(1, NZ)])
        part = pl.pallas_call(
            plane_kernel,
            out_shape=jax.ShapeDtypeStruct((NZ, ROWS, F), BF),
            in_specs=[VMEM],
            out_specs=VMEM,
            compiler_params=params(),
            cost_estimate=pl.CostEstimate(flops=2_000_000_000, bytes_accessed=3_000_000, transcendentals=0),
            name="plane_sum",
        )(planes)
        rings = exchange(part, "z").astype(F32)
        block = jnp.concatenate([block] + [shift(block, "y", NY, -k) for k in range(1, NY)], axis=0)
        block, part = lax.optimization_barrier((block, part))
        near_block = jnp.concatenate(
            [block] + [shift(block, "x", NX, -k) for k in range(1, NX)], axis=0
        )
        weight_grad = pl.pallas_call(
            place_kernel,
            out_shape=jax.ShapeDtypeStruct((F, F), F32),
            in_specs=[SMEM, VMEM, VMEM],
            out_specs=VMEM,
            compiler_params=params(),
            cost_estimate=pl.CostEstimate(flops=1_000_000, bytes_accessed=2_000_000, transcendentals=0),
            name="place",
        )(coord, near_block, swap(near_block))
        feature_grad = jnp.sum(rings, axis=0).astype(BF)
    return (feature_grad, weight_grad)


def solution(mesh):
    grid = Mesh(mesh.devices.reshape(NX, NY, NZ, NC), ("x", "y", "z", "c"))
    split = P(("x", "y", "z", "c"))
    return jax.shard_map(
        per_device,
        mesh=grid,
        in_specs=(split, P(), split, split, split, split, split, split),
        out_specs=(split, P()),
        check_vma=False,
    )
```

```python
import functools
import math

import jax
import jax.numpy as jnp
from jax import lax
from jax.experimental import pallas as pl
from jax.experimental.pallas import tpu as pltpu
from jax.sharding import Mesh, PartitionSpec as P

NX, NY, NZ, NC = 4, 4, 8, 2
NDEV = NY * NZ * NC
ROWS = 64
F = 512
CAP = 512
BF = jnp.bfloat16
F32 = jnp.float32
I32 = jnp.int32
POS = 4096.0
SUB = 256
SUBS = 8
NT = (((1,), (1,)), ((), ()))
TN = (((0,), (0,)), ((), ()))
VMEM = pl.BlockSpec(memory_space=pltpu.VMEM)
SMEM = pl.BlockSpec(memory_space=pltpu.SMEM)
ANY = pl.BlockSpec(memory_space=pl.ANY)


TOKEN = jax.ShapeDtypeStruct((8, 128), F32)


def params(mib=16):
    return pltpu.CompilerParams(vmem_limit_bytes=mib << 20)


def activation(values):
    return jax.nn.gelu(values)


def bucket_kernel(owner_ref, row_ref, out_ref, token_ref, acc):
    token_ref[...] = jnp.zeros_like(token_ref)
    total = owner_ref.shape[1]
    positives = total // 5
    step = SUB * SUBS
    tri = (
        lax.broadcasted_iota(I32, (SUB, SUB), 0) < lax.broadcasted_iota(I32, (SUB, SUB), 1)
    ).astype(BF)
    acc[...] = jnp.zeros_like(acc)
    base = jnp.zeros((NDEV, 1), F32)
    for end in range(2):

        def body(j, base, end=end):
            ranks, parts = [], [[], [], [], []]
            for s in range(SUBS):
                start = pl.multiple_of(j * step + s * SUB, SUB)
                here = pl.ds(start, SUB)
                own = owner_ref[end : end + 1, here]
                same = lax.broadcasted_iota(I32, (NDEV, SUB), 0) == own
                hot = same.astype(F32)
                prefix = jnp.dot(hot.astype(BF), tri, preferred_element_type=F32)
                ranks.append(jnp.sum(hot * (prefix + base), axis=0, keepdims=True))
                base = base + jnp.sum(hot, axis=1, keepdims=True)
                place = start + lax.broadcasted_iota(I32, (1, SUB), 1)
                weight = jnp.where(place < positives, POS, 1.0)
                values = [
                    weight,
                    row_ref[end : end + 1, here].astype(F32),
                    owner_ref[1 - end : 2 - end, here].astype(F32),
                    row_ref[1 - end : 2 - end, here].astype(F32),
                ]
                for v in range(4):
                    parts[v].append((hot * values[v]).astype(BF))
            left = jnp.concatenate([jnp.concatenate(p, axis=1) for p in parts], axis=0)
            rank = jnp.concatenate(ranks, axis=1).astype(I32)
            right = (lax.broadcasted_iota(I32, (CAP, step), 0) == rank).astype(F32).astype(BF)
            acc[...] += lax.dot_general(left, right, NT, preferred_element_type=F32)
            return base

        base = lax.fori_loop(0, total // step, body, base)
    for v in range(4):
        out_ref[:, v * CAP : (v + 1) * CAP] = acc[v * NDEV : (v + 1) * NDEV, :].astype(BF)


def count_kernel(coord_ref, recv_ref, near_ref, far_ref, token_ref, left_at, right_at, weight_at):
    token_ref[...] = jnp.zeros_like(token_ref)
    y, c = coord_ref[0], coord_ref[1]
    weight_at[...] = recv_ref[:, 0:CAP].astype(F32)
    own_row = recv_ref[:, CAP : 2 * CAP].astype(F32).astype(I32)
    owner = recv_ref[:, 2 * CAP : 3 * CAP].astype(F32).astype(I32)
    row = recv_ref[:, 3 * CAP : 4 * CAP].astype(F32).astype(I32)
    piece = ((owner & 1) ^ c) * NY + (((owner >> 4) - y) & (NY - 1))
    left_at[...] = piece * ROWS + own_row
    right_at[...] = ((owner >> 1) & (NZ - 1)) * ROWS + row
    near_ref[...] = jnp.zeros_like(near_ref)
    far_ref[...] = jnp.zeros_like(far_ref)
    group = 7
    groups = NDEV // group
    size = NY * ROWS

    def add(start, count):
        spots = lax.broadcasted_iota(I32, (CAP, CAP), 0)
        left, right = [], []
        for s in range(count):
            here = pl.ds(start + s, 1)
            left.append(jnp.where(spots == left_at[here, :], weight_at[here, :], 0.0).astype(BF))
            right.append(jnp.where(spots == right_at[here, :], 1.0, 0.0).astype(BF))
        total = lax.dot_general(
            jnp.concatenate(left, axis=1), jnp.concatenate(right, axis=1), NT, preferred_element_type=F32
        )
        ones = jnp.floor(total * (1.0 / POS))
        both = total - (POS - 1.0) * ones
        near_ref[0] += both[:size]
        near_ref[1] += ones[:size]
        far_ref[0] += both[size:]
        far_ref[1] += ones[size:]

    def body(g, carry):
        add(g * group, group)
        return carry

    lax.fori_loop(0, groups, body, 0)
    add(groups * group, NDEV - groups * group)


def grad_kernel(scale, _, own_ref, count_ref, *refs):
    pieces, rest, out_ref = refs[:NY], refs[NY:-1], refs[-1]
    own = own_ref[...]
    total = rest[0][...] if rest else jnp.zeros((ROWS, F), F32)
    for k in range(NY):
        nodes = pieces[k][...]
        score = lax.dot_general(own, nodes, NT, preferred_element_type=F32) / math.sqrt(F)
        here = slice(k * ROWS, (k + 1) * ROWS)
        grad = (count_ref[0, here, :] * jax.nn.sigmoid(score) - count_ref[1, here, :]) * scale
        high = grad.astype(BF)
        low = (grad - high.astype(F32)).astype(BF)
        total += jnp.dot(high, nodes, preferred_element_type=F32)
        total += jnp.dot(low, nodes, preferred_element_type=F32)
    out_ref[...] = total


def tiles_kernel(meta_ref, own_ref, other_ref, sum_ref, token_ref, acc):
    token_ref[...] = jnp.zeros_like(token_ref)
    slots = own_ref.shape[0]
    acc[...] = jnp.zeros_like(acc)
    for part, tiles_ref in enumerate((own_ref, other_ref)):

        def body(s, carry, part=part, tiles_ref=tiles_ref):
            rows = pl.ds(pl.multiple_of(meta_ref[part, s] * ROWS, ROWS), ROWS)
            dst = meta_ref[part, slots + s]
            columns = pl.ds(pl.multiple_of(part * 256 + dst * 128, 128), 128)
            acc[rows, columns] += tiles_ref[s].astype(F32)
            return carry

        lax.fori_loop(0, meta_ref[part, 2 * slots], body, 0)

    def split(k, carry):
        rows = pl.ds(pl.multiple_of(k * 128, 128), 128)
        sum_ref[rows, :] = acc[rows, :].astype(BF)
        return carry

    lax.fori_loop(0, acc.shape[0] // 128, split, 0)


def spread_kernel(coord_ref, _, weight_ref, tile_ref, *refs):
    pre_refs, out_ref, pre = refs[: NC * NX], refs[-2], refs[-1]
    x = coord_ref[2]
    for k in range(NC * NX):
        dc, dx = k // NX, k % NX
        place = pl.multiple_of((dc * NX + ((x + dx) & (NX - 1))) * ROWS, ROWS)
        pre[pl.ds(place, ROWS), :] = pre_refs[k][:, :F]
    agg = lax.dot_general(pre[...], weight_ref[...], NT, preferred_element_type=F32).astype(BF)
    size = NZ * ROWS
    for k in range(NY):
        rows = slice(k * size, (k + 1) * size)
        part = jnp.dot(tile_ref[rows, :], agg, preferred_element_type=F32)
        out_ref[k] = part.astype(BF)


def terms_kernel(coord_ref, _, *refs):
    part_refs, out_refs = refs[: NC * NX], refs[NC * NX : -2]
    token_ref, terms = refs[-2:]
    token_ref[...] = jnp.zeros_like(token_ref)
    y, c = coord_ref[0], coord_ref[1]
    node = jnp.concatenate([ref[:, F:] for ref in part_refs], axis=0)
    pre = jnp.concatenate([ref[:, :F] for ref in part_refs], axis=0)
    terms[...] = lax.dot_general(node, pre, TN, preferred_element_type=F32)
    size = ROWS // NY
    for k in range(NY):
        start = c * ROWS + ((y + k) & (NY - 1)) * size
        out_refs[k][...] = terms[pl.ds(pl.multiple_of(start, size), size), :]


def plane_kernel(in_ref, out_ref):
    value = in_ref[0].astype(F32)
    for k in range(1, NY):
        value = value + in_ref[k].astype(F32)
    for k in range(NZ):
        out_ref[k] = value[k * ROWS : (k + 1) * ROWS, :].astype(BF)


def place_kernel(coord_ref, near_ref, far_ref, out_ref):
    y, c, x = coord_ref[0], coord_ref[1], coord_ref[2]
    size = ROWS // NY
    for dc, ref in enumerate((near_ref, far_ref)):
        for dx in range(NX):
            for dy in range(NY):
                start = (((x + dx) & (NX - 1)) * NC + (c ^ dc)) * ROWS + ((y + dy) & (NY - 1)) * size
                here = (dx * NY + dy) * size
                out_ref[pl.ds(pl.multiple_of(start, size), size), :] = ref[here : here + size, :]


def share_kernel(coord_ref, *refs):
    in_refs, out_ref, parts = refs[:NZ], refs[NZ], refs[-1]
    z = coord_ref[3]
    for k in range(NZ):
        parts[(z + k) & (NZ - 1)] = in_refs[k][...]
    value = parts[0]
    for k in range(1, NZ):
        value = value + parts[k]
    out_ref[...] = value


def swap(values):
    return lax.ppermute(values, "c", [(0, 1), (1, 0)])


def shift(values, axis, size, step):
    return lax.ppermute(values, axis, [(i, (i + step) % size) for i in range(size)])


def exchange(values, axes):
    return lax.all_to_all(values, axes, 0, 0, tiled=True)


def gather(values, axes, size):
    return exchange(jnp.broadcast_to(values[None], (size,) + values.shape), axes)


def pick(values, place):
    return lax.dynamic_index_in_dim(values, place, 0, keepdims=False)


def count(coord, received):
    half = jax.ShapeDtypeStruct((2, NY * ROWS, NZ * ROWS), F32)
    return pl.pallas_call(
        count_kernel,
        out_shape=[half, half, TOKEN],
        in_specs=[SMEM, VMEM],
        out_specs=[VMEM] * 3,
        scratch_shapes=[
            pltpu.VMEM((NDEV, CAP), I32),
            pltpu.VMEM((NDEV, CAP), I32),
            pltpu.VMEM((NDEV, CAP), F32),
        ],
        compiler_params=params(),
        cost_estimate=pl.CostEstimate(flops=24_000_000_000, bytes_accessed=2_400_000, transcendentals=0),
        name="count",
    )(coord, received)


def pair_grad(scale, token, own, counted, *arrays):
    return pl.pallas_call(
        functools.partial(grad_kernel, scale),
        out_shape=jax.ShapeDtypeStruct((ROWS, F), F32),
        in_specs=[ANY] + [VMEM] * (2 + len(arrays)),
        out_specs=VMEM,
        compiler_params=params(),
        cost_estimate=pl.CostEstimate(flops=3_000_000_000, bytes_accessed=3_000_000, transcendentals=131072),
        name="pair_grad",
    )(token, own, counted, *arrays)


def per_device(node_aggregate, weight, tiles, tile_src, tile_dst, tile_count, pair_owner, pair_row):
    pair_total = pair_owner.shape[0]
    slots = tiles.shape[0]
    c = lax.axis_index("c")
    coord = jnp.stack(
        [lax.axis_index("y"), c, lax.axis_index("x"), lax.axis_index("z")]
    ).astype(I32)

    with jax.named_scope("hidden"):
        pre_act = jnp.dot(node_aggregate, weight, preferred_element_type=F32)
        hidden, act_back = jax.vjp(activation, pre_act)
        hidden_b = hidden.astype(BF)

    with jax.named_scope("pair_exchange"):
        ends, token = pl.pallas_call(
            bucket_kernel,
            out_shape=[jax.ShapeDtypeStruct((NDEV, 4 * CAP), BF), TOKEN],
            in_specs=[VMEM, VMEM],
            out_specs=[VMEM, VMEM],
            scratch_shapes=[pltpu.VMEM((4 * NDEV, CAP), F32)],
            compiler_params=params(),
            cost_estimate=pl.CostEstimate(flops=9_000_000_000, bytes_accessed=400_000, transcendentals=0),
            name="bucket",
        )(pair_owner.T, pair_row.T)
        ends = ends.reshape(NDEV, 2, 2 * CAP)
        ring = gather(hidden_b, "z", NZ).reshape(NZ * ROWS, F)
        ring, ends = lax.optimization_barrier((ring, ends))
        planes = [ring] + [shift(ring, "y", NY, -k) for k in range(1, NY)]
        received = exchange(ends, ("y", "z", "c")).reshape(NDEV, 4 * CAP)
        near, far, token = count(coord, received)

    with jax.named_scope("tile_matrix"):
        halves = tiles.reshape(slots, 2, ROWS, tiles.shape[2]).transpose(1, 0, 2, 3)
        own_half = pick(halves, c)
        other_half = swap(pick(halves, 1 - c))
        meta = jnp.concatenate([tile_src, tile_dst, tile_count]).astype(I32)
        metas = jnp.stack([meta, swap(meta)])
        far_ring = swap(ring)
        *planes, token = lax.optimization_barrier((*planes, token))
        far_planes = [far_ring] + [swap(plane) for plane in planes[1:]]
    with jax.named_scope("hidden_grad"):
        scale = ROWS / (2.0 * pair_total)
        hidden_grad = pair_grad(scale, token, hidden_b, near, *planes)
        hidden_grad = pair_grad(scale, token, hidden_b, far, *far_planes, hidden_grad)
        pre_grad = act_back(hidden_grad)[0].astype(BF)
        pre_grad, metas = lax.optimization_barrier((pre_grad, metas))

    with jax.named_scope("spread"):
        tile_matrix, tile_token = pl.pallas_call(
            tiles_kernel,
            out_shape=[jax.ShapeDtypeStruct((NY * NZ * ROWS, 512), BF), TOKEN],
            in_specs=[SMEM, VMEM, VMEM],
            out_specs=[VMEM] * 2,
            scratch_shapes=[pltpu.VMEM((NY * NZ * ROWS, 512), F32)],
            compiler_params=params(),
            cost_estimate=pl.CostEstimate(flops=3_000_000_000, bytes_accessed=5_000_000, transcendentals=0),
            name="tile_sum",
        )(metas, own_half, other_half)
        width = F // NX
        x = lax.axis_index("x")
        rows = []
        for k in range(NX):
            there = ((x - k) & (NX - 1)) * width
            node = lax.dynamic_slice_in_dim(node_aggregate, there, width, axis=1)
            rows.append(jnp.concatenate([pre_grad, node], axis=1))
        along_x = [shift(rows[k], "x", NX, -k) for k in range(1, NX)]
        *along_x, tile_token = lax.optimization_barrier((*along_x, tile_token))
        parts = [rows[0]] + along_x
        parts = parts + [swap(part) for part in parts]
        *terms, token = pl.pallas_call(
            terms_kernel,
            out_shape=[jax.ShapeDtypeStruct((ROWS // NY, F), F32)] * NY + [TOKEN],
            in_specs=[SMEM, ANY] + [VMEM] * (NC * NX),
            out_specs=[VMEM] * (NY + 1),
            scratch_shapes=[pltpu.VMEM((NC * ROWS, F), F32)],
            compiler_params=params(),
            cost_estimate=pl.CostEstimate(flops=1_000_000_000, bytes_accessed=700_000, transcendentals=0),
            name="weight_terms",
        )(coord, tile_token, *parts)
        others = [shift(terms[k], "y", NY, k) for k in range(1, NY)]
        send = pl.pallas_call(
            spread_kernel,
            out_shape=jax.ShapeDtypeStruct((NY, NZ * ROWS, F), BF),
            in_specs=[SMEM, ANY] + [VMEM] * (2 + NC * NX),
            out_specs=VMEM,
            scratch_shapes=[pltpu.VMEM((NC * NX * ROWS, F), BF)],
            compiler_params=params(),
            cost_estimate=pl.CostEstimate(flops=5_000_000_000, bytes_accessed=8_000_000, transcendentals=0),
            name="spread",
        )(coord, token, weight, tile_matrix, *parts)

    with jax.named_scope("sums"):
        *others, send = lax.optimization_barrier((*others, send))
        planes = exchange(send, "y")
        share = terms[0]
        for other in others:
            share = share + other
        block = pl.pallas_call(
            share_kernel,
            out_shape=jax.ShapeDtypeStruct((ROWS // NY, F), F32),
            in_specs=[SMEM] + [VMEM] * NZ,
            out_specs=VMEM,
            scratch_shapes=[pltpu.VMEM((NZ, ROWS // NY, F), F32)],
            compiler_params=params(),
            cost_estimate=pl.CostEstimate(flops=1_000_000, bytes_accessed=300_000, transcendentals=0),
            name="share_sum",
        )(coord, share, *[shift(share, "z", NZ, -k) for k in range(1, NZ)])
        part = pl.pallas_call(
            plane_kernel,
            out_shape=jax.ShapeDtypeStruct((NZ, ROWS, F), BF),
            in_specs=[VMEM],
            out_specs=VMEM,
            compiler_params=params(),
            cost_estimate=pl.CostEstimate(flops=2_000_000_000, bytes_accessed=3_000_000, transcendentals=0),
            name="plane_sum",
        )(planes)
        rings = exchange(part, "z").astype(F32)
        block = jnp.concatenate([block] + [shift(block, "y", NY, -k) for k in range(1, NY)], axis=0)
        block, part = lax.optimization_barrier((block, part))
        near_block = jnp.concatenate(
            [block] + [shift(block, "x", NX, -k) for k in range(1, NX)], axis=0
        )
        weight_grad = pl.pallas_call(
            place_kernel,
            out_shape=jax.ShapeDtypeStruct((F, F), F32),
            in_specs=[SMEM, VMEM, VMEM],
            out_specs=VMEM,
            compiler_params=params(),
            cost_estimate=pl.CostEstimate(flops=1_000_000, bytes_accessed=2_000_000, transcendentals=0),
            name="place",
        )(coord, near_block, swap(near_block))
        feature_grad = jnp.sum(rings, axis=0).astype(BF)
    return (feature_grad, weight_grad)


def solution(mesh):
    grid = Mesh(mesh.devices.reshape(NX, NY, NZ, NC), ("x", "y", "z", "c"))
    split = P(("x", "y", "z", "c"))
    return jax.shard_map(
        per_device,
        mesh=grid,
        in_specs=(split, P(), split, split, split, split, split, split),
        out_specs=(split, P()),
        check_vma=False,
    )
```
